256 devices in a mesh: dp: 8 (over y, core), expert: 32 (over z, x).
Axes of the slice: x: 4, y: 4, z: 8, core: 2. Of those that a mesh axis runs over, the one named last changes fastest.
Arguments:
- tokens: bfloat16 [73728, 2048], P(('dp', 'expert')), may hold values from -36 to 36
- cotangent: bfloat16 [73728, 2048], P(('dp', 'expert')), may hold values from -1.796875 to 1.796875
- expert_ids: int32 [24576, 2], P(('dp', 'expert')), may hold values from 0 to 31, all different within a row; in each aligned block of 96 rows (0 to 95, 96 to 191, ...) at most 12 rows name the same one
- votes: int32 [24576, 2], P(('dp', 'expert')), may hold values from 1 to 8
- pool_weight: float32 [3, 2048], replicated, may hold values from 0.2 to 1
- norm_gain: float32 [2048], replicated, may hold values from 0.5 to 2
- up_gain: float32 [3, 2048], replicated, may hold values from 0.5 to 1.5
- gate_weight: bfloat16 [32, 1024, 2048], P('expert', 'dp'), may hold values from -0.125 to 0.125
- up_weight: bfloat16 [32, 1024, 2048], P('expert', 'dp'), may hold values from -0.125 to 0.125
- down_weight: bfloat16 [32, 1024, 2048], P('expert', 'dp'), may hold values from -0.1875 to 0.1875
Outputs:
- layer_out: bfloat16 [73728, 2048], P(('dp', 'expert'))
- tokens_grad: bfloat16 [73728, 2048], P(('dp', 'expert'))
- gate_grad: float32 [32, 1024, 2048], P('expert', 'dp')
- up_grad: float32 [32, 1024, 2048], P('expert', 'dp')
- down_grad: float32 [32, 1024, 2048], P('expert', 'dp')
The draws below stay inside these ranges and needn't reach their ends.
Inputs may be any that keep to these rules, and one draw needn't show every extreme that they name: `expert_ids`: each row names 2 different experts. In every aligned block of 96 rows (the rows of one device) no expert is named by more than 12 rows, a bound that some block reaches.
All inputs are finite; a program needn't handle non-finite values.
Results may differ from the reference program's by a relative error of at most 0.015.
Values may be sent and summed in bfloat16 or wider, within the bound.
No kernel may reach another device: no remote copies, remote signals or barrier semaphores. Data moves between devices by JAX's collectives and lax.ppermute only.
A program may use at most 128 MiB of HBM per device.

```python
import math
import jax
import jax.numpy as jnp
import numpy as np
from jax import lax

D = 2048
FF = 1024
SHORT = 3
TOP = 2
S_DEV = 96
EXPERTS = 32
CAP = 12
SROWS = 24576
TOKENS = 73728
N_DP = 8
N_EXPERT = 32
DEVICES = 256


def draw_tokens(key, part):
    key = jax.random.fold_in(key, 11)
    key_base, key_rows, key_cols = jax.random.split(key, 3)
    base_values = jnp.clip(jax.random.normal(key_base, (TOKENS, D), jnp.float32), -4.0, 4.0)
    row_scales = jnp.exp(jax.random.uniform(key_rows, (TOKENS, 1), jnp.float32, math.log(0.3), math.log(3.0)))
    col_scales = jnp.exp(jax.random.uniform(key_cols, (1, D), jnp.float32, math.log(0.3), math.log(3.0)))
    return (base_values * row_scales * col_scales).astype(jnp.bfloat16)


def touch_ends(drawn, key, least, high):
    spot = [jax.random.randint(jax.random.fold_in(key, axis), (), 0, length) for axis, length in enumerate(drawn.shape)]
    widest = drawn.shape.index(max(drawn.shape))
    next_to = spot[:widest] + [(spot[widest] + 1) % drawn.shape[widest]] + spot[widest + 1:]
    return drawn.at[tuple(spot)].set(least).at[tuple(next_to)].set(high)


def block_scale(rng, shape, cuts, smallest, high):
    gain, own = 1.0, jax.random.fold_in(rng, 6)
    for axis_at, shards_of in cuts:
        heights = jnp.exp(jax.random.uniform(jax.random.fold_in(own, axis_at), (shards_of,), jnp.float32, smallest / len(cuts), high / len(cuts)))
        gain = gain * jnp.repeat(heights, shape[axis_at] // shards_of).reshape([-1 if axis == axis_at else 1 for axis in range(len(shape))])
    return gain


def shared_out(own_key, own, number, rows, amount, top, reach, slope):
    sequence = jax.random.permutation(own_key, amount)
    packed, ordinary = shares(amount, rows * top, reach, slope, True), shares(amount, rows * top, reach, slope, False)
    places = jnp.arange(amount)

    def named(sizes, rotation):
        used = int((sizes > 0).sum())
        fixed = max(1, used // 4)
        passed = fixed + (places - fixed + rotation * (used - fixed)) % max(1, amount - fixed)
        return jnp.zeros((amount,), jnp.int32).at[sequence[jnp.where(places < fixed, places, passed)]].set(jnp.asarray(sizes, jnp.int32))

    sizes = jnp.where(number % 4 == 0, named(packed, number // 4), named(ordinary, number - number // 4 - 1))
    mixed = jax.random.permutation(jax.random.fold_in(own, 3), amount)
    source_of, taker = mixed[0:amount // 2 * 2:2], mixed[1:amount // 2 * 2:2]
    slack = jnp.minimum(sizes[source_of] - 1, reach - sizes[taker]) // 2
    slack = jnp.where((source_of == sequence[0]) | (taker == sequence[0]) | (sizes[taker] == 0), 0, jnp.maximum(slack, 0))
    passed = jax.random.randint(jax.random.fold_in(own, 4), (amount // 2,), 0, 1 << 20) % (slack + 1)
    sizes = sizes.at[source_of].add(-passed).at[taker].add(passed)
    members = jnp.searchsorted(jnp.cumsum(sizes), jnp.arange(rows * top), side="right").astype(jnp.int32)
    listing = members.reshape(top, rows).T
    listing = listing[jax.random.permutation(jax.random.fold_in(own, 1), rows)]
    rotation = jax.random.randint(jax.random.fold_in(own, 2), (rows, 1), 0, top)
    return jnp.take_along_axis(listing, (jnp.arange(top)[None, :] + rotation) % top, axis=1)


def shares(amount, total, reach, lean, full):
    loads = [(1 << 20) // math.isqrt(standing ** lean) + 1 for standing in range(1, amount + 1)]
    largest = reach if full else min(reach, max(-(-total // amount), total * loads[0] // sum(loads)))
    least = 1 if total - largest >= amount - 1 else 0
    given, surplus = [largest] + [least] * (amount - 1), total - largest - least * (amount - 1)
    while surplus > 0:
        candidates = [i for i in range(1, amount) if given[i] < largest] or [i for i in range(1, amount) if given[i] < reach]
        mass, left = sum([loads[i] for i in candidates]), surplus
        for i in candidates:
            extra = min(reach - given[i], max(1, left * loads[i] // mass), surplus)
            given[i] = given[i] + extra
            surplus = surplus - extra
    return np.array(given)


def bell_draw(stream_key, shape, deviation, most, pieces=(), kind=jnp.bfloat16):
    values = deviation * jax.random.normal(stream_key, shape, jnp.float32)
    if pieces:
        values = values * block_scale(stream_key, shape, pieces, -0.22, 0.18)
    return jnp.clip(values, -most, most).astype(kind)


def setup_inputs(seed: int = 0) -> dict:
    key_list = jax.random.split(jax.random.key(seed), 11)
    tokens = draw_tokens(jax.random.fold_in(key_list[10], 71), 0)
    cotangent = bell_draw(key_list[1], (TOKENS, D), 0.3, 1.796875, ((0, 256),))
    expert_ids_keys = jax.random.split(jax.random.fold_in(key_list[2], 1), SROWS // S_DEV)
    expert_ids_turns = jax.random.permutation(jax.random.fold_in(key_list[2], 3), SROWS // S_DEV)
    expert_ids = jax.vmap(lambda own, number: shared_out(jax.random.fold_in(key_list[2], 2), own, number, S_DEV, EXPERTS, TOP, CAP, 2))(expert_ids_keys, expert_ids_turns).reshape((SROWS, TOP))
    votes = touch_ends(jax.random.randint(key_list[3], (SROWS, TOP), 1, 9), jax.random.fold_in(key_list[3], 1), 1, 8).astype(jnp.int32)
    pool_weight = jnp.clip(jax.random.uniform(key_list[4], (SHORT, D), jnp.float32, 0.2, 1.0), 0.2, 1.0)
    norm_gain = jnp.clip(jnp.exp(jax.random.uniform(key_list[5], (D,), jnp.float32, math.log(0.5), math.log(2.0))), 0.5, 2.0)
    up_gain = jnp.clip(jax.random.uniform(key_list[6], (SHORT, D), jnp.float32, 0.5, 1.5), 0.5, 1.5)
    gate_weight = bell_draw(key_list[7], (EXPERTS, FF, D), D ** -0.5, 0.125, ((0, 32), (1, 8)))
    up_weight = bell_draw(key_list[8], (EXPERTS, FF, D), D ** -0.5, 0.125, ((0, 32), (1, 8)))
    down_weight = bell_draw(key_list[9], (EXPERTS, FF, D), FF ** -0.5, 0.1875, ((0, 32), (1, 8)))
    return {"tokens": tokens, "cotangent": cotangent, "expert_ids": expert_ids, "votes": votes, "pool_weight": pool_weight, "norm_gain": norm_gain, "up_gain": up_gain, "gate_weight": gate_weight, "up_weight": up_weight, "down_weight": down_weight}


def slot_table(routed, experts, capacity):
    flat_ids = routed.reshape(-1)
    onehot = (flat_ids[:, None] == jnp.arange(experts, dtype=jnp.int32)[None, :]).astype(jnp.int32)
    earlier = jnp.cumsum(onehot, axis=0) - onehot
    ranking = lax.optimization_barrier(jnp.sum(earlier * onehot, axis=1))
    return (flat_ids * capacity + ranking).astype(jnp.int32)

def expert_pass(inputs, grads_in, w_gate, w_up, w_down):
    contract = (((1,), (1,)), ((), ()))
    pre_gate = lax.dot_general(inputs, w_gate, contract, preferred_element_type=jnp.float32)
    pre_up = lax.dot_general(inputs, w_up, contract, preferred_element_type=jnp.float32)
    sigmoid_gate = jax.nn.sigmoid(pre_gate)
    active = pre_gate * sigmoid_gate
    hidden = (active * pre_up).astype(jnp.bfloat16)
    outputs = jnp.dot(hidden, w_down, preferred_element_type=jnp.float32).astype(jnp.bfloat16)
    d_hidden = lax.dot_general(grads_in, w_down, contract, preferred_element_type=jnp.float32)
    d_gate = (d_hidden * pre_up * sigmoid_gate * (1.0 + pre_gate * (1.0 - sigmoid_gate))).astype(jnp.bfloat16)
    d_up = (d_hidden * active).astype(jnp.bfloat16)
    d_inputs = (jnp.dot(d_gate, w_gate, preferred_element_type=jnp.float32) + jnp.dot(d_up, w_up, preferred_element_type=jnp.float32)).astype(jnp.bfloat16)
    return (outputs, d_inputs, d_gate, d_up, hidden)

def place_rows(slot_row, row_values):
    return jnp.zeros((EXPERTS * CAP, D), jnp.bfloat16).at[slot_row].set(row_values)

def pick_rows(table_rows, slot_row):
    return table_rows[slot_row]

def arrange(sent):
    return sent.reshape(N_DP, N_EXPERT, EXPERTS, CAP, D).transpose(2, 0, 1, 3, 4)

def unarrange(arrived):
    return arrived.transpose(1, 2, 0, 3, 4).reshape(DEVICES, EXPERTS * CAP, D)

def one_expert(expert_item):
    x_in, g_in, w_gate, w_up, w_down = expert_item
    x_flat = x_in.reshape(-1, D)
    g_flat = g_in.reshape(-1, D)
    outputs, d_inputs, d_gate, d_up, hidden = expert_pass(x_flat, g_flat, w_gate, w_up, w_down)
    group_rows = N_EXPERT * CAP
    results = []
    for left_side, right_side in ((d_gate, x_flat), (d_up, x_flat), (hidden, g_flat)):
        running = jnp.zeros((FF, D), jnp.float32)
        for dp_group in range(N_DP):
            first_row = dp_group * group_rows
            last_row = first_row + group_rows
            partial_term = jnp.dot(left_side[first_row:last_row].T, right_side[first_row:last_row], preferred_element_type=jnp.float32)
            running = running + lax.optimization_barrier(partial_term.astype(jnp.bfloat16)).astype(jnp.float32)
        results.append(running)
    return (outputs.reshape(x_in.shape), d_inputs.reshape(x_in.shape), results[0], results[1], results[2])

def reference(tokens, cotangent, expert_ids, votes, pool_weight, norm_gain, up_gain, gate_weight, up_weight, down_weight):
    short_total = DEVICES * S_DEV
    grouped = tokens.reshape(short_total, SHORT, D).astype(jnp.float32)
    short = lax.optimization_barrier(jnp.sum(grouped * pool_weight[None], axis=1))
    inv_rms = lax.rsqrt(lax.optimization_barrier(jnp.mean(short * short, axis=1, keepdims=True)) + 1e-06)
    scaled = short * inv_rms
    normed = (scaled * norm_gain[None]).astype(jnp.bfloat16)
    vote_values = votes.astype(jnp.float32)
    gates = vote_values / lax.optimization_barrier(jnp.sum(vote_values, axis=1, keepdims=True))
    d_mix = lax.optimization_barrier(jnp.sum(cotangent.reshape(short_total, SHORT, D).astype(jnp.float32) * up_gain[None], axis=1))
    grad_in = (gates[:, :, None] * d_mix[:, None, :]).astype(jnp.bfloat16)
    slot_ids = jax.vmap(partial_table)(expert_ids.reshape(DEVICES, S_DEV, TOP))
    x_rows = jnp.broadcast_to(normed[:, None, :], (short_total, TOP, D)).reshape(DEVICES, S_DEV * TOP, D)
    g_rows = grad_in.reshape(DEVICES, S_DEV * TOP, D)
    x_send = jax.vmap(place_rows)(slot_ids, x_rows)
    g_send = jax.vmap(place_rows)(slot_ids, g_rows)
    y_all, dx_all, gate_grad, up_grad, down_grad = lax.map(one_expert, (arrange(x_send), arrange(g_send), gate_weight, up_weight, down_weight))
    y_tok = jax.vmap(pick_rows)(unarrange(y_all), slot_ids).reshape(short_total, TOP, D).astype(jnp.float32)
    dx_tok = jax.vmap(pick_rows)(unarrange(dx_all), slot_ids).reshape(short_total, TOP, D).astype(jnp.float32)
    mixture = lax.optimization_barrier(jnp.sum(gates[:, :, None] * y_tok, axis=1))
    layer_out = (up_gain[None] * mixture[:, None, :]).astype(jnp.bfloat16).reshape(short_total * SHORT, D)
    d_normed = lax.optimization_barrier(jnp.sum(dx_tok, axis=1))
    d_scaled = d_normed * norm_gain[None]
    d_short = inv_rms * (d_scaled - scaled * lax.optimization_barrier(jnp.mean(d_scaled * scaled, axis=1, keepdims=True)))
    tokens_grad = (pool_weight[None] * d_short[:, None, :]).astype(jnp.bfloat16).reshape(short_total * SHORT, D)
    return (layer_out, tokens_grad, gate_grad, up_grad, down_grad)

def partial_table(routed):
    return slot_table(routed, EXPERTS, CAP)
```

```python
import functools

import jax
import jax.numpy as jnp
from jax import lax
from jax.experimental import pallas as pl
from jax.experimental.pallas import tpu as pltpu
from jax.sharding import PartitionSpec as P

BF = jnp.bfloat16
F32 = jnp.float32
VMEM_LIMIT = 60 * 1024 * 1024


def nn(a, b):
    return jnp.dot(a, b, preferred_element_type=F32)


def nt(a, b):
    return lax.dot_general(a, b, (((1,), (1,)), ((), ())), preferred_element_type=F32)


def tn(a, b):
    return lax.dot_general(a, b, (((0,), (0,)), ((), ())), preferred_element_type=F32)


def iota(shape, axis):
    return lax.broadcasted_iota(jnp.int32, shape, axis)


def slots_and_gates(ids_ref, votes_ref, experts, capacity):
    rows = ids_ref.shape[0]
    ids = ids_ref[...]
    first, second = ids[:, 0:1], ids[:, 1:2]
    names = iota((rows, experts), 1)
    hot0 = (names == first).astype(F32)
    hot1 = (names == second).astype(F32)
    earlier = (iota((rows, rows), 0) > iota((rows, rows), 1)).astype(BF)
    before = nn(earlier, (hot0 + hot1).astype(BF))
    rank0 = jnp.sum(before * hot0, axis=1, keepdims=True).astype(jnp.int32)
    rank1 = jnp.sum(before * hot1, axis=1, keepdims=True).astype(jnp.int32)
    votes = votes_ref[...].astype(F32)
    total = votes[:, 0:1] + votes[:, 1:2]
    slot0 = first * (2 * capacity) + rank0
    slot1 = second * (2 * capacity) + rank1
    return slot0, slot1, votes[:, 0:1] / total, votes[:, 1:2] / total


def pick(rows, factor, j):
    shape = (rows, rows * factor)
    return (iota(shape, 1) == iota(shape, 0) * factor + j).astype(BF)


def before_kernel(experts, capacity, tokens, cotangent, ids, votes, pool, norm, gain, send, scaled_out, inv_out):
    rows = ids.shape[0]
    factor = tokens.shape[0] // rows
    slot0, slot1, gate0, gate1 = slots_and_gates(ids, votes, experts, capacity)
    tok = tokens[...]
    cot = cotangent[...]
    short = None
    d_mix = None
    for j in range(factor):
        sel = pick(rows, factor, j)
        a = nn(sel, tok) * pool[j : j + 1, :]
        b = nn(sel, cot) * gain[j : j + 1, :]
        short = a if short is None else short + a
        d_mix = b if d_mix is None else d_mix + b
    inv = lax.rsqrt(jnp.mean(short * short, axis=1, keepdims=True) + 1e-06)
    scaled = short * inv
    scaled_out[...] = scaled
    inv_out[...] = jnp.broadcast_to(inv, inv_out.shape)
    values = jnp.concatenate(
        [
            (scaled * norm[...]).astype(BF),
            (gate0 * d_mix).astype(BF),
            (gate1 * d_mix).astype(BF),
        ],
        axis=0,
    )
    place = iota((rows, send.shape[0]), 1)
    spread = jnp.concatenate(
        [
            jnp.where((place == slot0) | (place == slot1), 1.0, 0.0).astype(BF),
            jnp.where(place == slot0 + capacity, 1.0, 0.0).astype(BF),
            jnp.where(place == slot1 + capacity, 1.0, 0.0).astype(BF),
        ],
        axis=0,
    )
    send[...] = tn(spread, values).astype(BF)


def split_matrix(rows, capacity):
    half = rows // 2
    r = iota((rows, rows), 0)
    c = iota((rows, rows), 1)
    kind = (r >= half).astype(jnp.int32)
    within = r - kind * half
    source = (within // capacity) * (2 * capacity) + kind * capacity + within % capacity
    return (c == source).astype(BF)


def expert_kernel(capacity, group, arrived, weights, back, partials, xs, gs, y_sum, dx_sum):
    step = pl.program_id(0)
    steps = pl.num_programs(0)
    half = group // 2
    groups = arrived.shape[0] // group

    @pl.when(step == 0)
    def _():
        sel = split_matrix(group, capacity)
        for i in range(groups):
            both = nn(sel, arrived[i * group : (i + 1) * group, :]).astype(BF)
            xs[i * half : (i + 1) * half, :] = both[:half]
            gs[i * half : (i + 1) * half, :] = both[half:]

    x = xs[...]
    g = gs[...]
    parts = weights.shape[0]
    w_gate = jnp.concatenate([weights[p, 0] for p in range(parts)], axis=0)
    w_up = jnp.concatenate([weights[p, 1] for p in range(parts)], axis=0)
    w_down = jnp.concatenate([weights[p, 2] for p in range(parts)], axis=0)
    pre_gate = nt(x, w_gate)
    pre_up = nt(x, w_up)
    d_hidden = nt(g, w_down)
    sig = jax.nn.sigmoid(pre_gate)
    active = pre_gate * sig
    hidden = (active * pre_up).astype(BF)
    d_gate = (d_hidden * pre_up * sig * (1.0 + pre_gate * (1.0 - sig))).astype(BF)
    d_up = (d_hidden * active).astype(BF)
    y = nn(hidden, w_down)
    dx = nn(d_gate, w_gate) + nn(d_up, w_up)

    @pl.when(step == 0)
    def _():
        y_sum[...] = y
        dx_sum[...] = dx

    @pl.when(step > 0)
    def _():
        y_sum[...] += y
        dx_sum[...] += dx

    width = w_gate.shape[0] // parts
    for m, (left, right) in enumerate(((d_gate, x), (d_up, x), (hidden, g))):
        both = tn(left, right).astype(BF)
        for p in range(parts):
            partials[p, m] = both[p * width : (p + 1) * width]

    @pl.when(step == steps - 1)
    def _():
        sel = split_matrix(group, capacity)
        for i in range(groups):
            both = jnp.concatenate(
                [
                    y_sum[i * half : (i + 1) * half, :].astype(BF),
                    dx_sum[i * half : (i + 1) * half, :].astype(BF),
                ],
                axis=0,
            )
            back[i * group : (i + 1) * group, :] = tn(sel, both).astype(BF)


def after_kernel(experts, capacity, table, scaled_in, inv_in, ids, votes, pool, norm, gain, out, grad):
    rows = ids.shape[0]
    factor = out.shape[0] // rows
    slot0, slot1, gate0, gate1 = slots_and_gates(ids, votes, experts, capacity)
    place = iota((rows, table.shape[0]), 1)
    grad0, grad1 = slot0 + capacity, slot1 + capacity
    sel = jnp.concatenate(
        [
            jnp.where(place == slot0, 1.0, 0.0).astype(BF),
            jnp.where(place == slot1, 1.0, 0.0).astype(BF),
            jnp.where((place == grad0) | (place == grad1), 1.0, 0.0).astype(BF),
        ],
        axis=0,
    )
    found = nn(sel, table[...])
    mixture = gate0 * found[:rows] + gate1 * found[rows : 2 * rows]
    d_scaled = found[2 * rows :] * norm[...]
    scaled = scaled_in[...]
    inv = inv_in[:, 0:1]
    d_short = inv * (d_scaled - scaled * jnp.mean(d_scaled * scaled, axis=1, keepdims=True))
    outs = jnp.concatenate([(gain[j : j + 1, :] * mixture).astype(BF) for j in range(factor)], axis=0)
    grads = jnp.concatenate([(pool[j : j + 1, :] * d_short).astype(BF) for j in range(factor)], axis=0)
    shape = (rows * factor, rows * factor)
    r, c = iota(shape, 0), iota(shape, 1)
    mix = (c == (r % factor) * rows + r // factor).astype(BF)
    out[...] = nn(mix, outs).astype(BF)
    grad[...] = nn(mix, grads).astype(BF)


def shards(
    tokens,
    cotangent,
    expert_ids,
    votes,
    pool_weight,
    norm_gain,
    up_gain,
    gate_weight,
    up_weight,
    down_weight,
):
    experts = lax.axis_size("expert")
    shares = lax.axis_size("dp")
    rows, top = expert_ids.shape
    width = tokens.shape[1]
    hidden = gate_weight.shape[1]
    capacity = 2 * rows * top // experts
    slots = 2 * experts * capacity
    params = pltpu.CompilerParams(vmem_limit_bytes=VMEM_LIMIT)

    mine = jnp.concatenate([gate_weight, up_weight, down_weight], axis=0)
    weights = lax.all_gather(mine, "dp", axis=0, tiled=False)

    norm = norm_gain[None]
    send, scaled, inv = pl.pallas_call(
        functools.partial(before_kernel, experts, capacity),
        out_shape=(
            jax.ShapeDtypeStruct((slots, width), BF),
            jax.ShapeDtypeStruct((rows, width), F32),
            jax.ShapeDtypeStruct((rows, 128), F32),
        ),
        compiler_params=params,
        name="before",
    )(tokens, cotangent, expert_ids, votes, pool_weight, norm, up_gain)

    arrived = lax.all_to_all(send, "expert", split_axis=0, concat_axis=0, tiled=True)

    parts = 2
    group = 16 * capacity
    half_rows = slots // 2
    back, partials = pl.pallas_call(
        functools.partial(expert_kernel, capacity, group),
        grid=(shares // parts,),
        in_specs=[
            pl.BlockSpec((slots, width), lambda i: (0, 0)),
            pl.BlockSpec((parts, 3, hidden, width), lambda i: (i, 0, 0, 0)),
        ],
        out_specs=[
            pl.BlockSpec((slots, width), lambda i: (0, 0)),
            pl.BlockSpec((parts, 3, hidden, width), lambda i: (i, 0, 0, 0)),
        ],
        out_shape=(
            jax.ShapeDtypeStruct((slots, width), BF),
            jax.ShapeDtypeStruct((shares, 3, hidden, width), BF),
        ),
        scratch_shapes=[
            pltpu.VMEM((half_rows, width), BF),
            pltpu.VMEM((half_rows, width), BF),
            pltpu.VMEM((half_rows, width), F32),
            pltpu.VMEM((half_rows, width), F32),
        ],
        compiler_params=params,
        name="experts",
    )(arrived, weights)

    summed = lax.psum_scatter(partials, "dp", scatter_dimension=0, tiled=False)
    returned = lax.all_to_all(back, "expert", split_axis=0, concat_axis=0, tiled=True)

    layer_out, tokens_grad = pl.pallas_call(
        functools.partial(after_kernel, experts, capacity),
        out_shape=(
            jax.ShapeDtypeStruct(tokens.shape, BF),
            jax.ShapeDtypeStruct(tokens.shape, BF),
        ),
        compiler_params=params,
        name="after",
    )(returned, scaled, inv, expert_ids, votes, pool_weight, norm, up_gain)
    grads = summed.astype(F32)
    return (layer_out, tokens_grad, grads[0:1], grads[1:2], grads[2:3])


def solution(mesh):
    rows = P(("dp", "expert"), None)
    held = P("expert", "dp", None)
    return jax.shard_map(
        shards,
        mesh=mesh,
        in_specs=(rows, rows, rows, rows, P(), P(), P(), held, held, held),
        out_specs=(rows, rows, held, held, held),
        check_vma=False,
    )
```

```python
import functools

import jax
import jax.numpy as jnp
from jax import lax
from jax.experimental import pallas as pl
from jax.experimental.pallas import tpu as pltpu
from jax.sharding import PartitionSpec as P

BF = jnp.bfloat16
F32 = jnp.float32
MIB = 1024 * 1024
EDGE_LIMIT = 60 * MIB
EXPERTS_LIMIT = 60 * MIB
SUMS_LIMIT = 60 * MIB


def nn(a, b):
    return jnp.dot(a, b, preferred_element_type=F32)


def nt(a, b):
    return lax.dot_general(a, b, (((1,), (1,)), ((), ())), preferred_element_type=F32)


def tn(a, b):
    return lax.dot_general(a, b, (((0,), (0,)), ((), ())), preferred_element_type=F32)


def iota(shape, axis):
    return lax.broadcasted_iota(jnp.int32, shape, axis)


def slots_and_gates(ids_ref, votes_ref, experts, capacity):
    rows = ids_ref.shape[1]
    ids = ids_ref[...].astype(F32).T.astype(jnp.int32)
    first, second = ids[:, 0:1], ids[:, 1:2]
    names = iota((rows, experts), 1)
    hot0 = (names == first).astype(F32)
    hot1 = (names == second).astype(F32)
    earlier = (iota((rows, rows), 0) > iota((rows, rows), 1)).astype(BF)
    before = nn(earlier, (hot0 + hot1).astype(BF))
    rank0 = jnp.sum(before * hot0, axis=1, keepdims=True).astype(jnp.int32)
    rank1 = jnp.sum(before * hot1, axis=1, keepdims=True).astype(jnp.int32)
    votes = votes_ref[...].astype(F32).T
    total = votes[:, 0:1] + votes[:, 1:2]
    slot0 = first * (2 * capacity) + rank0
    slot1 = second * (2 * capacity) + rank1
    return slot0, slot1, votes[:, 0:1] / total, votes[:, 1:2] / total


def pick(rows, factor, j):
    shape = (rows, rows * factor)
    return (iota(shape, 1) == iota(shape, 0) * factor + j).astype(BF)


def pack_kernel(w_gate, w_up, w_down, first, second, held, in_sem, out_sem):
    width = w_gate.shape[1]
    half = first.shape[0]
    loads = [pltpu.make_async_copy(src.at[0], held.at[pl.ds(m * width, width)], in_sem.at[m]) for m, src in enumerate((w_gate, w_up, w_down))]
    stores = [pltpu.make_async_copy(held.at[pl.ds(h * half, half)], dst, out_sem.at[h]) for h, dst in enumerate((first, second))]
    for copy in loads:
        copy.start()
    for copy in loads[:2]:
        copy.wait()
    stores[0].start()
    loads[2].wait()
    stores[1].start()
    for copy in stores:
        copy.wait()


def before_kernel(experts, capacity, tokens, cotangent, ids, votes, pool, norm, gain, send, scaled_out, inv_out):
    rows = ids.shape[1]
    factor = tokens.shape[0] // rows
    slot0, slot1, gate0, gate1 = slots_and_gates(ids, votes, experts, capacity)
    tok = tokens[...]
    cot = cotangent[...]
    short = None
    d_mix = None
    for j in range(factor):
        sel = pick(rows, factor, j)
        a = nn(sel, tok) * pool[j : j + 1, :]
        b = nn(sel, cot) * gain[j : j + 1, :]
        short = a if short is None else short + a
        d_mix = b if d_mix is None else d_mix + b
    inv = lax.rsqrt(jnp.mean(short * short, axis=1, keepdims=True) + 1e-06)
    scaled = short * inv
    scaled_out[...] = scaled
    inv_out[...] = jnp.broadcast_to(inv, inv_out.shape)
    values = jnp.concatenate(
        [
            (scaled * norm[...]).astype(BF),
            (gate0 * d_mix).astype(BF),
            (gate1 * d_mix).astype(BF),
        ],
        axis=0,
    )
    place = iota((rows, send.shape[0]), 1)
    spread = jnp.concatenate(
        [
            jnp.where((place == slot0) | (place == slot1), 1.0, 0.0).astype(BF),
            jnp.where(place == slot0 + capacity, 1.0, 0.0).astype(BF),
            jnp.where(place == slot1 + capacity, 1.0, 0.0).astype(BF),
        ],
        axis=0,
    )
    send[...] = tn(spread, values).astype(BF)


def split_matrix(rows, capacity):
    half = rows // 2
    r = iota((rows, rows), 0)
    c = iota((rows, rows), 1)
    kind = (r >= half).astype(jnp.int32)
    within = r - kind * half
    source = (within // capacity) * (2 * capacity) + kind * capacity + within % capacity
    return (c == source).astype(BF)


def experts_kernel(capacity, group, cols, arrived, *refs):
    halves, refs = refs[:16], refs[16:]
    back, x_out, g_out, left_out, theirs, mixed, w, xs, gs, acts, lefts, in_sem, w_sem, out_sem, back_sem, part_sem = refs
    half = group // 2
    groups = arrived.shape[0] // group
    pieces, three, model = w.shape
    width = three // 3
    full = pieces * width
    parts = 2
    step = parts * width
    loads = [
        pltpu.make_async_copy(arrived.at[pl.ds(i * group, group)], mixed.at[pl.ds(i * group, group)], in_sem.at[i])
        for i in range(groups)
    ]
    held = [
        pltpu.make_async_copy(src, w.at[i // 2, pl.ds((i % 2) * (three // 2), three // 2)], w_sem.at[i]) for i, src in enumerate(halves)
    ]
    for copy in loads + held:
        copy.start()
    sel = split_matrix(group, capacity)
    for i in range(groups):
        loads[i].wait()
        both = nn(sel, mixed[i * group : (i + 1) * group, :]).astype(BF)
        xs[i * half : (i + 1) * half, :] = both[:half]
        gs[i * half : (i + 1) * half, :] = both[half:]
    outs = [pltpu.make_async_copy(xs, x_out, out_sem.at[0]), pltpu.make_async_copy(gs, g_out, out_sem.at[1])]
    for copy in outs:
        copy.start()
    for c in range(pieces // parts):
        for copy in held[2 * c * parts : 2 * (c + 1) * parts]:
            copy.wait()
        mine = slice(c * parts, (c + 1) * parts)
        x = xs[...]
        pre_gate = nt(x, w[mine, 0:width].reshape(step, model))
        pre_up = nt(x, w[mine, width : 2 * width].reshape(step, model))
        d_hidden = nt(gs[...], w[mine, 2 * width :].reshape(step, model))
        sig = jax.nn.sigmoid(pre_gate)
        active = pre_gate * sig
        hidden = active * pre_up
        d_gate = d_hidden * pre_up * sig * (1.0 + pre_gate * (1.0 - sig))
        d_up = d_hidden * active
        at = slice(c * step, (c + 1) * step)
        for m, part in enumerate((d_gate, d_up, hidden)):
            rounded = part.astype(BF)
            acts[m, :, at] = rounded
            lefts[m, at, :] = rounded.T
    copy = pltpu.make_async_copy(lefts.at[:, pl.ds(0, full // 2)], left_out, out_sem.at[2])
    copy.start()
    outs.append(copy)
    for n in range(model // cols):
        at = slice(n * cols, (n + 1) * cols)
        y = nn(acts[2], w[:, 2 * width :, at].reshape(full, cols)).astype(BF)
        dx = nn(acts[0], w[:, 0:width, at].reshape(full, cols)) + nn(acts[1], w[:, width : 2 * width, at].reshape(full, cols))
        dx = dx.astype(BF)
        for i in range(groups):
            both = jnp.concatenate([y[i * half : (i + 1) * half], dx[i * half : (i + 1) * half]], axis=0)
            mixed[i * group : (i + 1) * group, at] = tn(sel, both).astype(BF)
        copy = pltpu.make_async_copy(mixed.at[:, pl.ds(n * cols, cols)], back.at[:, pl.ds(n * cols, cols)], back_sem.at[n])
        copy.start()
        outs.append(copy)
    other = pieces // 2
    for m, right in enumerate((xs, xs, gs)):
        span = slice(m * width, (m + 1) * width)
        w[other:, span, :] = nn(lefts[m, full // 2 :, :], right[...]).astype(BF).reshape(other, width, model)
        copy = pltpu.make_async_copy(w.at[pl.ds(other, other), pl.ds(m * width, width)], theirs.at[:, pl.ds(m * width, width)], part_sem.at[m])
        copy.start()
        outs.append(copy)
    for copy in outs:
        copy.wait()


def experts_call(arrived, halves, capacity):
    slots, width = arrived.shape
    three = 2 * halves[0].shape[0]
    pieces = len(halves) // 2
    full = pieces * three // 3
    rows = slots // 2
    group = 16 * capacity
    cols = width // 2
    hbm = pl.BlockSpec(memory_space=pl.ANY)
    return pl.pallas_call(
        functools.partial(experts_kernel, capacity, group, cols),
        in_specs=[hbm] * (1 + len(halves)),
        out_specs=[hbm] * 5,
        out_shape=(
            jax.ShapeDtypeStruct((slots, width), BF),
            jax.ShapeDtypeStruct((rows, width), BF),
            jax.ShapeDtypeStruct((rows, width), BF),
            jax.ShapeDtypeStruct((3, full // 2, rows), BF),
            jax.ShapeDtypeStruct((pieces // 2, three, width), BF),
        ),
        scratch_shapes=[
            pltpu.VMEM((slots, width), BF),
            pltpu.VMEM((pieces, three, width), BF),
            pltpu.VMEM((rows, width), BF),
            pltpu.VMEM((rows, width), BF),
            pltpu.VMEM((3, rows, full), BF),
            pltpu.VMEM((3, full, rows), BF),
            pltpu.SemaphoreType.DMA((slots // group,)),
            pltpu.SemaphoreType.DMA((len(halves),)),
            pltpu.SemaphoreType.DMA((3,)),
            pltpu.SemaphoreType.DMA((width // cols,)),
            pltpu.SemaphoreType.DMA((3,)),
        ],
        compiler_params=pltpu.CompilerParams(vmem_limit_bytes=EXPERTS_LIMIT),
        cost_estimate=pl.CostEstimate(flops=15 * rows * full * width, bytes_accessed=8 * slots * width, transcendentals=rows * full),
        name="experts",
    )(arrived, *halves)


def sums_kernel(x_in, g_in, left_in, theirs, p0a, p0b, p1a, p1b, p2a, p2b, p3a, p3b, x, g, left, add, p, in_sem, add_sem, out_sem):
    pieces, three, model = p.shape
    width = three // 3
    part = width // 2
    dsts = ((p0a, p0b), (p1a, p1b), (p2a, p2b), (p3a, p3b))
    loads = [
        pltpu.make_async_copy(left_in, left, in_sem.at[0]),
        pltpu.make_async_copy(x_in, x, in_sem.at[1]),
        pltpu.make_async_copy(g_in, g, in_sem.at[2]),
    ]
    order = (2, 1, 3, 0)
    terms = {k: pltpu.make_async_copy(theirs.at[k], add.at[k], add_sem.at[k]) for k in order}
    for copy in loads[:2] + [terms[2]] + loads[2:] + [terms[k] for k in order[1:]]:
        copy.start()
    for copy in loads:
        copy.wait()
    outs = []
    for k in order:
        terms[k].wait()
        for m, right in enumerate((x, x, g)):
            span = slice(m * width, (m + 1) * width)
            total = nn(left[m, k * width : (k + 1) * width, :], right[...]) + add[k, span].astype(F32)
            p[k, span] = total.astype(BF)
        for h in range(2):
            copy = pltpu.make_async_copy(p.at[k, pl.ds(3 * h * part, 3 * part)], dsts[k][h], out_sem.at[k, h])
            copy.start()
            outs.append(copy)
    for copy in outs:
        copy.wait()


def sums_call(x, g, left, theirs):
    rows, width = x.shape
    pieces, three, _ = theirs.shape
    full = left.shape[1]
    hbm = pl.BlockSpec(memory_space=pl.ANY)
    return pl.pallas_call(
        sums_kernel,
        in_specs=[hbm] * 4,
        out_specs=[hbm] * (2 * pieces),
        out_shape=tuple(jax.ShapeDtypeStruct((three // 2, width), BF) for _ in range(2 * pieces)),
        scratch_shapes=[
            pltpu.VMEM(x.shape, BF),
            pltpu.VMEM(g.shape, BF),
            pltpu.VMEM(left.shape, BF),
            pltpu.VMEM(theirs.shape, BF),
            pltpu.VMEM(theirs.shape, BF),
            pltpu.SemaphoreType.DMA((3,)),
            pltpu.SemaphoreType.DMA((pieces,)),
            pltpu.SemaphoreType.DMA((pieces, 2)),
        ],
        compiler_params=pltpu.CompilerParams(vmem_limit_bytes=SUMS_LIMIT),
        cost_estimate=pl.CostEstimate(flops=6 * rows * full * width, bytes_accessed=20 * rows * width, transcendentals=0),
        name="sums",
    )(x, g, left, theirs)


def after_kernel(
    experts, capacity, table, scaled_in, inv_in, ids, votes, pool, norm, gain, q0a, q0b, q1a, q1b, q2a, q2b, out, grad, o_gate, o_up, o_down, q, total, q_sem, o_sem
):
    part = q.shape[1] // 2
    loads = [
        pltpu.make_async_copy(src, q.at[k // 2, pl.ds((k % 2) * part, part)], q_sem.at[k]) for k, src in enumerate((q0a, q0b, q1a, q1b, q2a, q2b))
    ]
    for copy in loads:
        copy.start()
    rows = ids.shape[1]
    factor = out.shape[0] // rows
    slot0, slot1, gate0, gate1 = slots_and_gates(ids, votes, experts, capacity)
    place = iota((rows, table.shape[0]), 1)
    grad0, grad1 = slot0 + capacity, slot1 + capacity
    sel = jnp.concatenate(
        [
            jnp.where(place == slot0, 1.0, 0.0).astype(BF),
            jnp.where(place == slot1, 1.0, 0.0).astype(BF),
            jnp.where((place == grad0) | (place == grad1), 1.0, 0.0).astype(BF),
        ],
        axis=0,
    )
    found = nn(sel, table[...])
    mixture = gate0 * found[:rows] + gate1 * found[rows : 2 * rows]
    d_scaled = found[2 * rows :] * norm[...]
    scaled = scaled_in[...]
    inv = inv_in[:, 0:1]
    d_short = inv * (d_scaled - scaled * jnp.mean(d_scaled * scaled, axis=1, keepdims=True))
    outs = jnp.concatenate([(gain[j : j + 1, :] * mixture).astype(BF) for j in range(factor)], axis=0)
    grads = jnp.concatenate([(pool[j : j + 1, :] * d_short).astype(BF) for j in range(factor)], axis=0)
    shape = (rows * factor, rows * factor)
    r, c = iota(shape, 0), iota(shape, 1)
    mix = (c == (r % factor) * rows + r // factor).astype(BF)
    out[...] = nn(mix, outs).astype(BF)
    grad[...] = nn(mix, grads).astype(BF)
    stores = []
    for copy in loads:
        copy.wait()
    width = total.shape[1]
    for m, dst in enumerate((o_gate, o_up, o_down)):
        at = slice(m * width, (m + 1) * width)
        terms = [q[k, at].astype(F32) for k in range(3)]
        total[m] = terms[0] + terms[1] + terms[2]
        copy = pltpu.make_async_copy(total.at[m], dst.at[0], o_sem.at[m])
        copy.start()
        stores.append(copy)
    for copy in stores:
        copy.wait()


def shards(
    tokens,
    cotangent,
    expert_ids,
    votes,
    pool_weight,
    norm_gain,
    up_gain,
    gate_weight,
    up_weight,
    down_weight,
):
    ring = lax.axis_size("y")
    experts = lax.axis_size("z") * lax.axis_size("x")
    rows, top = expert_ids.shape
    width = tokens.shape[1]
    hidden = gate_weight.shape[1]
    capacity = 2 * rows * top // experts
    slots = 2 * experts * capacity
    params = pltpu.CompilerParams(vmem_limit_bytes=EDGE_LIMIT)
    vmem = pl.BlockSpec(memory_space=pltpu.VMEM)
    hbm = pl.BlockSpec(memory_space=pl.ANY)
    norm = norm_gain[None]
    ids, counts = expert_ids.T, votes.T

    def move(a, k):
        return lax.ppermute(a, "y", [(i, (i + k) % ring) for i in range(ring)])

    def swap(a):
        return lax.ppermute(a, "core", [(0, 1), (1, 0)])

    def exchange(a):
        return lax.all_to_all(a, ("z", "x"), split_axis=0, concat_axis=0, tiled=True)

    up, down = 1, ring - 1
    h0, h1 = pl.pallas_call(
        pack_kernel,
        in_specs=[hbm] * 3,
        out_specs=[hbm] * 2,
        out_shape=(jax.ShapeDtypeStruct((3 * hidden // 2, width), BF),) * 2,
        scratch_shapes=[pltpu.VMEM((3 * hidden, width), BF), pltpu.SemaphoreType.DMA((3,)), pltpu.SemaphoreType.DMA((2,))],
        compiler_params=params,
        name="pack",
    )(gate_weight, up_weight, down_weight)
    u0, d1 = move(h0, up), move(h1, down)
    t0, t1 = move(u0, up), move(d1, down)
    u1, d0 = move(h1, up), move(h0, down)
    halves = [h0, h1, u0, u1, t0, t1, d0, d1]
    halves = halves + [swap(a) for a in halves]

    send, scaled, inv = pl.pallas_call(
        functools.partial(before_kernel, experts, capacity),
        out_shape=(
            jax.ShapeDtypeStruct((slots, width), BF),
            jax.ShapeDtypeStruct((rows, width), F32),
            jax.ShapeDtypeStruct((rows, 128), F32),
        ),
        compiler_params=params,
        name="before",
    )(tokens, cotangent, ids, counts, pool_weight, norm, up_gain)

    arrived = exchange(send)
    back, x, g, left, theirs = experts_call(arrived, halves, capacity)
    returned = exchange(back)
    p0a, p0b, p1a, p1b, p2a, p2b, p3a, p3b = sums_call(x, g, left, swap(theirs))
    r1b, r3a = move(p1b, down), move(p3a, up)
    r1a = move(p1a + move(p2a, down), down)
    r3b = move(p3b + move(p2b, up), up)
    parts = (p0a, p0b, r1a, r1b, r3a, r3b)

    shape = jax.ShapeDtypeStruct(tokens.shape, BF)
    held = jax.ShapeDtypeStruct((1, hidden, width), F32)
    return pl.pallas_call(
        functools.partial(after_kernel, experts, capacity),
        in_specs=[vmem] * 8 + [hbm] * 6,
        out_specs=[vmem] * 2 + [hbm] * 3,
        out_shape=(shape, shape, held, held, held),
        scratch_shapes=[
            pltpu.VMEM((3, 3 * hidden, width), BF),
            pltpu.VMEM((3, hidden, width), F32),
            pltpu.SemaphoreType.DMA((6,)),
            pltpu.SemaphoreType.DMA((3,)),
        ],
        compiler_params=params,
        name="after",
    )(returned, scaled, inv, ids, counts, pool_weight, norm, up_gain, *parts)


def solution(mesh):
    sizes = (mesh.shape["dp"] // 2, 2, mesh.shape["expert"] // 4, 4)
    mesh = jax.sharding.Mesh(mesh.devices.reshape(sizes), ("y", "core", "z", "x"))
    rows = P(("y", "core", "z", "x"), None)
    held = P(("z", "x"), ("y", "core"), None)
    return jax.shard_map(
        shards,
        mesh=mesh,
        in_specs=(rows, rows, rows, rows, P(), P(), P(), held, held, held),
        out_specs=(rows, rows, held, held, held),
        check_vma=False,
    )
```

```python
import functools

import jax
import jax.numpy as jnp
from jax import lax
from jax.experimental import pallas as pl
from jax.experimental.pallas import tpu as pltpu
from jax.sharding import PartitionSpec as P

BF = jnp.bfloat16
F32 = jnp.float32
MIB = 1024 * 1024
EDGE_LIMIT = 60 * MIB
AFTER_LIMIT = 52 * MIB
EXPERTS_LIMIT = 50 * MIB
SUMS_LIMIT = 60 * MIB


def nn(a, b):
    return jnp.dot(a, b, preferred_element_type=F32)


def nt(a, b):
    return lax.dot_general(a, b, (((1,), (1,)), ((), ())), preferred_element_type=F32)


def tn(a, b):
    return lax.dot_general(a, b, (((0,), (0,)), ((), ())), preferred_element_type=F32)


def iota(shape, axis):
    return lax.broadcasted_iota(jnp.int32, shape, axis)


def slots_and_gates(ids_ref, votes_ref, experts, capacity):
    rows = ids_ref.shape[1]
    ids = ids_ref[...].astype(F32).T.astype(jnp.int32)
    first, second = ids[:, 0:1], ids[:, 1:2]
    names = iota((rows, experts), 1)
    hot0 = (names == first).astype(F32)
    hot1 = (names == second).astype(F32)
    earlier = (iota((rows, rows), 0) > iota((rows, rows), 1)).astype(BF)
    before = nn(earlier, (hot0 + hot1).astype(BF))
    rank0 = jnp.sum(before * hot0, axis=1, keepdims=True).astype(jnp.int32)
    rank1 = jnp.sum(before * hot1, axis=1, keepdims=True).astype(jnp.int32)
    votes = votes_ref[...].astype(F32).T
    total = votes[:, 0:1] + votes[:, 1:2]
    slot0 = first * (2 * capacity) + rank0
    slot1 = second * (2 * capacity) + rank1
    return slot0, slot1, votes[:, 0:1] / total, votes[:, 1:2] / total


def pick(rows, factor, j):
    shape = (rows, rows * factor)
    return (iota(shape, 1) == iota(shape, 0) * factor + j).astype(BF)


def pack_kernel(w_gate, w_up, w_down, first, second, held, in_sem, out_sem):
    width = w_gate.shape[1]
    half = first.shape[0]
    loads = [pltpu.make_async_copy(src.at[0], held.at[pl.ds(m * width, width)], in_sem.at[m]) for m, src in enumerate((w_gate, w_up, w_down))]
    stores = [pltpu.make_async_copy(held.at[pl.ds(h * half, half)], dst, out_sem.at[h]) for h, dst in enumerate((first, second))]
    for copy in loads:
        copy.start()
    for copy in loads[:2]:
        copy.wait()
    stores[0].start()
    loads[2].wait()
    stores[1].start()
    for copy in stores:
        copy.wait()


def before_kernel(experts, capacity, tokens, cotangent, ids, votes, pool, norm, gain, send, scaled_out, inv_out):
    rows = ids.shape[1]
    factor = tokens.shape[0] // rows
    slot0, slot1, gate0, gate1 = slots_and_gates(ids, votes, experts, capacity)
    tok = tokens[...]
    cot = cotangent[...]
    short = None
    d_mix = None
    for j in range(factor):
        sel = pick(rows, factor, j)
        a = nn(sel, tok) * pool[j : j + 1, :]
        b = nn(sel, cot) * gain[j : j + 1, :]
        short = a if short is None else short + a
        d_mix = b if d_mix is None else d_mix + b
    inv = lax.rsqrt(jnp.mean(short * short, axis=1, keepdims=True) + 1e-06)
    scaled = short * inv
    scaled_out[...] = scaled
    inv_out[...] = jnp.broadcast_to(inv, inv_out.shape)
    values = jnp.concatenate(
        [
            (scaled * norm[...]).astype(BF),
            (gate0 * d_mix).astype(BF),
            (gate1 * d_mix).astype(BF),
        ],
        axis=0,
    )
    place = iota((rows, send.shape[0]), 1)
    spread = jnp.concatenate(
        [
            jnp.where((place == slot0) | (place == slot1), 1.0, 0.0).astype(BF),
            jnp.where(place == slot0 + capacity, 1.0, 0.0).astype(BF),
            jnp.where(place == slot1 + capacity, 1.0, 0.0).astype(BF),
        ],
        axis=0,
    )
    send[...] = tn(spread, values).astype(BF)


def split_matrix(rows, capacity):
    half = rows // 2
    r = iota((rows, rows), 0)
    c = iota((rows, rows), 1)
    kind = (r >= half).astype(jnp.int32)
    within = r - kind * half
    source = (within // capacity) * (2 * capacity) + kind * capacity + within % capacity
    return (c == source).astype(BF)


def experts_kernel(capacity, group, cols, arrived, *refs):
    halves, refs = refs[:16], refs[16:]
    back, packed, left_out, mixed, w, xs, gs, acts, lefts, in_sem, w_sem, out_sem, back_sem = refs
    half = group // 2
    groups = arrived.shape[0] // group
    pieces, three, model = w.shape
    width = three // 3
    full = pieces * width
    parts = 2
    step = parts * width
    loads = [
        pltpu.make_async_copy(arrived.at[pl.ds(i * group, group)], mixed.at[pl.ds(i * group, group)], in_sem.at[i])
        for i in range(groups)
    ]
    held = [
        pltpu.make_async_copy(src, w.at[i // 2, pl.ds((i % 2) * (three // 2), three // 2)], w_sem.at[i]) for i, src in enumerate(halves)
    ]
    chunk = 2 * parts
    for copy in loads + held[:chunk]:
        copy.start()
    sel = split_matrix(group, capacity)
    for i in range(groups):
        loads[i].wait()
        if i == 1:
            for copy in held[chunk : 2 * chunk]:
                copy.start()
        both = nn(sel, mixed[i * group : (i + 1) * group, :]).astype(BF)
        xs[i * half : (i + 1) * half, :] = both[:half]
        gs[i * half : (i + 1) * half, :] = both[half:]
    outs = [pltpu.make_async_copy(src, packed.at[:, pl.ds(i * model, model)], out_sem.at[i]) for i, src in enumerate((xs, gs))]
    for c in range(pieces // parts):
        for copy in held[c * chunk : (c + 1) * chunk]:
            copy.wait()
        if c == 0:
            for copy in outs:
                copy.start()
        for copy in held[(c + 2) * chunk : (c + 3) * chunk]:
            copy.start()
        mine = slice(c * parts, (c + 1) * parts)
        x = xs[...]
        pre_gate = nt(x, w[mine, 0:width].reshape(step, model))
        pre_up = nt(x, w[mine, width : 2 * width].reshape(step, model))
        d_hidden = nt(gs[...], w[mine, 2 * width :].reshape(step, model))
        sig = jax.nn.sigmoid(pre_gate)
        active = pre_gate * sig
        hidden = active * pre_up
        d_gate = d_hidden * pre_up * sig * (1.0 + pre_gate * (1.0 - sig))
        d_up = d_hidden * active
        at = slice(c * step, (c + 1) * step)
        for m, part in enumerate((d_gate, d_up, hidden)):
            rounded = part.astype(BF)
            acts[m, :, at] = rounded
            if 2 * c < pieces // parts:
                lefts[m, at, :] = rounded.T
    mine = full // 2
    last = [pltpu.make_async_copy(lefts, left_out, out_sem.at[2])]
    for m in range(3):
        theirs = packed.at[:, pl.ds(2 * model + m * mine, mine)]
        last.append(pltpu.make_async_copy(acts.at[m, :, pl.ds(mine, mine)], theirs, out_sem.at[3 + m]))
    for copy in last:
        copy.start()
    outs += last
    for n in range(model // cols):
        at = slice(n * cols, (n + 1) * cols)
        y = nn(acts[2], w[:, 2 * width :, at].reshape(full, cols)).astype(BF)
        dx = nn(acts[0], w[:, 0:width, at].reshape(full, cols)) + nn(acts[1], w[:, width : 2 * width, at].reshape(full, cols))
        dx = dx.astype(BF)
        for i in range(groups):
            both = jnp.concatenate([y[i * half : (i + 1) * half], dx[i * half : (i + 1) * half]], axis=0)
            mixed[i * group : (i + 1) * group, at] = tn(sel, both).astype(BF)
        copy = pltpu.make_async_copy(mixed.at[:, pl.ds(n * cols, cols)], back.at[:, pl.ds(n * cols, cols)], back_sem.at[n])
        copy.start()
        outs.append(copy)
    for copy in outs:
        copy.wait()


def experts_call(arrived, halves, capacity):
    slots, width = arrived.shape
    three = 2 * halves[0].shape[0]
    pieces = len(halves) // 2
    full = pieces * three // 3
    rows = slots // 2
    group = 16 * capacity
    cols = width // 2
    hbm = pl.BlockSpec(memory_space=pl.ANY)
    return pl.pallas_call(
        functools.partial(experts_kernel, capacity, group, cols),
        in_specs=[hbm] * (1 + len(halves)),
        out_specs=[hbm] * 3,
        out_shape=(
            jax.ShapeDtypeStruct((slots, width), BF),
            jax.ShapeDtypeStruct((rows, 2 * width + 3 * full // 2), BF),
            jax.ShapeDtypeStruct((3, full // 2, rows), BF),
        ),
        scratch_shapes=[
            pltpu.VMEM((slots, width), BF),
            pltpu.VMEM((pieces, three, width), BF),
            pltpu.VMEM((rows, width), BF),
            pltpu.VMEM((rows, width), BF),
            pltpu.VMEM((3, rows, full), BF),
            pltpu.VMEM((3, full // 2, rows), BF),
            pltpu.SemaphoreType.DMA((slots // group,)),
            pltpu.SemaphoreType.DMA((len(halves),)),
            pltpu.SemaphoreType.DMA((6,)),
            pltpu.SemaphoreType.DMA((width // cols,)),
        ],
        compiler_params=pltpu.CompilerParams(vmem_limit_bytes=EXPERTS_LIMIT),
        cost_estimate=pl.CostEstimate(flops=12 * rows * full * width, bytes_accessed=8 * slots * width, transcendentals=rows * full),
        name="experts",
    )(arrived, *halves)


def sums_kernel(jobs, packed_a, left_a, packed_b, d0, d1, d2, d3, x, g, left, acts, p, in_sem, out_sem):
    rows = left_a.shape[2]
    model = x.shape[1]
    mine = left.shape[1]
    _, three, cols = p.shape
    width = three // 3
    def load(src, dst, n):
        return pltpu.make_async_copy(src, dst, in_sem.at[n])

    lefts = load(left_a, left.at[:, :, pl.ds(0, rows)], 0)
    theirs = [load(packed_b.at[:, pl.ds(2 * model + m * mine, mine)], acts.at[m], 1 + m) for m in range(3)]
    sides = []
    for j, side in enumerate((x, g)):
        for i, src in enumerate((packed_a, packed_b)):
            sides.append(load(src.at[:, pl.ds(j * model, model)], side.at[pl.ds(i * rows, rows)], 4 + 2 * j + i))
    for copy in theirs + [lefts] + sides:
        copy.start()
    for m in range(3):
        theirs[m].wait()
        left[m, :, rows:] = acts[m].T
    lefts.wait()
    outs = []
    dsts = (d0, d1, d2, d3)
    for m, right in enumerate((x, x, g)):
        for copy in (sides[0:2], [], sides[2:4])[m]:
            copy.wait()
        for i, (half, pair) in enumerate(jobs):
            lhs = jnp.concatenate([left[m, k * width : (k + 1) * width, :] for k in pair], axis=0)
            found = nn(lhs, right[:, half * cols : (half + 1) * cols]).astype(BF)
            for j in range(2):
                p[2 * i + j, m * width : (m + 1) * width, :] = found[j * width : (j + 1) * width]
                at = pl.ds(m * width, width)
                copy = pltpu.make_async_copy(p.at[2 * i + j, at], dsts[2 * i + j].at[at], out_sem.at[m, 2 * i + j])
                copy.start()
                outs.append(copy)
    for copy in outs:
        copy.wait()


def sums_call(packed, left, theirs, pieces, jobs, name):
    _, mine, rows = left.shape
    width = (packed.shape[1] - 3 * mine) // 2
    three = 3 * mine // pieces
    hbm = pl.BlockSpec(memory_space=pl.ANY)
    return pl.pallas_call(
        functools.partial(sums_kernel, jobs),
        in_specs=[hbm] * 3,
        out_specs=[hbm] * 4,
        out_shape=(jax.ShapeDtypeStruct((three, width // 2), BF),) * 4,
        scratch_shapes=[
            pltpu.VMEM((2 * rows, width), BF),
            pltpu.VMEM((2 * rows, width), BF),
            pltpu.VMEM((3, mine, 2 * rows), BF),
            pltpu.VMEM((3, rows, mine), BF),
            pltpu.VMEM((4, three, width // 2), BF),
            pltpu.SemaphoreType.DMA((8,)),
            pltpu.SemaphoreType.DMA((3, 4)),
        ],
        compiler_params=pltpu.CompilerParams(vmem_limit_bytes=SUMS_LIMIT),
        cost_estimate=pl.CostEstimate(flops=6 * rows * mine * width, bytes_accessed=16 * rows * width, transcendentals=0),
        name=name,
    )(packed, left, theirs)


def grads_kernel(q0a, q0b, q1a, q1b, q2a, q2b, o_gate, o_up, o_down, q, total, q_sem, o_sem):
    cols = q.shape[2] // 2
    loads = [
        pltpu.make_async_copy(src, q.at[k // 2, :, pl.ds((k % 2) * cols, cols)], q_sem.at[k]) for k, src in enumerate((q0a, q0b, q1a, q1b, q2a, q2b))
    ]
    for copy in loads:
        copy.start()
    for copy in loads:
        copy.wait()
    stores = []
    width = total.shape[1]
    for m, dst in enumerate((o_gate, o_up, o_down)):
        at = slice(m * width, (m + 1) * width)
        terms = [q[k, at].astype(F32) for k in range(3)]
        total[m] = terms[0] + terms[1] + terms[2]
        copy = pltpu.make_async_copy(total.at[m], dst.at[0], o_sem.at[m])
        copy.start()
        stores.append(copy)
    for copy in stores:
        copy.wait()


def after_kernel(experts, capacity, table, scaled_in, inv_in, ids, votes, pool, norm, gain, out, grad):
    rows = ids.shape[1]
    factor = out.shape[0] // rows
    slot0, slot1, gate0, gate1 = slots_and_gates(ids, votes, experts, capacity)
    place = iota((rows, table.shape[0]), 1)
    grad0, grad1 = slot0 + capacity, slot1 + capacity
    sel = jnp.concatenate(
        [
            jnp.where(place == slot0, 1.0, 0.0).astype(BF),
            jnp.where(place == slot1, 1.0, 0.0).astype(BF),
            jnp.where((place == grad0) | (place == grad1), 1.0, 0.0).astype(BF),
        ],
        axis=0,
    )
    found = nn(sel, table[...])
    mixture = gate0 * found[:rows] + gate1 * found[rows : 2 * rows]
    d_scaled = found[2 * rows :] * norm[...]
    scaled = scaled_in[...]
    inv = inv_in[:, 0:1]
    d_short = inv * (d_scaled - scaled * jnp.mean(d_scaled * scaled, axis=1, keepdims=True))
    outs = jnp.concatenate([(gain[j : j + 1, :] * mixture).astype(BF) for j in range(factor)], axis=0)
    grads = jnp.concatenate([(pool[j : j + 1, :] * d_short).astype(BF) for j in range(factor)], axis=0)
    shape = (rows * factor, rows * factor)
    r, c = iota(shape, 0), iota(shape, 1)
    mix = (c == (r % factor) * rows + r // factor).astype(BF)
    out[...] = nn(mix, outs).astype(BF)
    grad[...] = nn(mix, grads).astype(BF)


def shards(
    tokens,
    cotangent,
    expert_ids,
    votes,
    pool_weight,
    norm_gain,
    up_gain,
    gate_weight,
    up_weight,
    down_weight,
):
    ring = lax.axis_size("y")
    experts = lax.axis_size("z") * lax.axis_size("x")
    rows, top = expert_ids.shape
    width = tokens.shape[1]
    hidden = gate_weight.shape[1]
    capacity = 2 * rows * top // experts
    slots = 2 * experts * capacity
    params = pltpu.CompilerParams(vmem_limit_bytes=EDGE_LIMIT)
    vmem = pl.BlockSpec(memory_space=pltpu.VMEM)
    hbm = pl.BlockSpec(memory_space=pl.ANY)
    norm = norm_gain[None]
    ids, counts = expert_ids.T, votes.T

    def move(a, k):
        return lax.ppermute(a, "y", [(i, (i + k) % ring) for i in range(ring)])

    def swap(a):
        return lax.ppermute(a, "core", [(0, 1), (1, 0)])

    def exchange(a):
        return lax.all_to_all(a, ("z", "x"), split_axis=0, concat_axis=0, tiled=True)

    up, down = 1, ring - 1
    h0, h1 = pl.pallas_call(
        pack_kernel,
        in_specs=[hbm] * 3,
        out_specs=[hbm] * 2,
        out_shape=(jax.ShapeDtypeStruct((3 * hidden // 2, width), BF),) * 2,
        scratch_shapes=[pltpu.VMEM((3 * hidden, width), BF), pltpu.SemaphoreType.DMA((3,)), pltpu.SemaphoreType.DMA((2,))],
        compiler_params=params,
        name="pack",
    )(gate_weight, up_weight, down_weight)
    u0, d1 = move(h0, up), move(h1, down)
    t0, t1 = move(u0, up), move(d1, down)
    u1, d0 = move(h1, up), move(h0, down)
    halves = [h0, h1, u0, u1, t0, t1, d0, d1]
    halves = halves + [swap(a) for a in halves]

    send, scaled, inv = pl.pallas_call(
        functools.partial(before_kernel, experts, capacity),
        out_shape=(
            jax.ShapeDtypeStruct((slots, width), BF),
            jax.ShapeDtypeStruct((rows, width), F32),
            jax.ShapeDtypeStruct((rows, 128), F32),
        ),
        compiler_params=params,
        name="before",
    )(tokens, cotangent, ids, counts, pool_weight, norm, up_gain)

    arrived = exchange(send)
    back, packed, left = experts_call(arrived, halves, capacity)
    theirs = swap(packed)
    returned = exchange(back)
    p2a, p3a, p1b, p2b = sums_call(packed, left, theirs, ring, ((0, (2, 3)), (1, (1, 2))), "sums_far")
    p0a, p1a, p3b, p0b = sums_call(packed, left, theirs, ring, ((0, (0, 1)), (1, (3, 0))), "sums_near")
    r1b, r3a = move(p1b, down), move(p3a, up)
    r1a = move(p1a + move(p2a, down), down)
    r3b = move(p3b + move(p2b, up), up)
    parts = (p0a, p0b, r1a, r1b, r3a, r3b)

    held = jax.ShapeDtypeStruct((1, hidden, width), F32)
    grads = pl.pallas_call(
        grads_kernel,
        in_specs=[hbm] * 6,
        out_specs=[hbm] * 3,
        out_shape=(held, held, held),
        scratch_shapes=[
            pltpu.VMEM((3, 3 * hidden, width), BF),
            pltpu.VMEM((3, hidden, width), F32),
            pltpu.SemaphoreType.DMA((6,)),
            pltpu.SemaphoreType.DMA((3,)),
        ],
        compiler_params=params,
        name="grads",
    )(*parts)

    shape = jax.ShapeDtypeStruct(tokens.shape, BF)
    layer_out, tokens_grad = pl.pallas_call(
        functools.partial(after_kernel, experts, capacity),
        out_shape=(shape, shape),
        compiler_params=pltpu.CompilerParams(vmem_limit_bytes=AFTER_LIMIT),
        name="after",
    )(returned, scaled, inv, ids, counts, pool_weight, norm, up_gain)
    return (layer_out, tokens_grad, *grads)


def solution(mesh):
    sizes = (mesh.shape["dp"] // 2, 2, mesh.shape["expert"] // 4, 4)
    mesh = jax.sharding.Mesh(mesh.devices.reshape(sizes), ("y", "core", "z", "x"))
    rows = P(("y", "core", "z", "x"), None)
    held = P(("z", "x"), ("y", "core"), None)
    return jax.shard_map(
        shards,
        mesh=mesh,
        in_specs=(rows, rows, rows, rows, P(), P(), P(), held, held, held),
        out_specs=(rows, rows, held, held, held),
        check_vma=False,
    )
```

```python
import functools

import jax
import jax.numpy as jnp
from jax import lax
from jax.experimental import pallas as pl
from jax.experimental.pallas import tpu as pltpu
from jax.sharding import PartitionSpec as P

BF = jnp.bfloat16
F32 = jnp.float32
MIB = 1024 * 1024
EDGE_LIMIT = 60 * MIB
AFTER_LIMIT = 52 * MIB
EXPERTS_LIMIT = 50 * MIB
SUMS_LIMIT = 60 * MIB


def nn(a, b):
    return jnp.dot(a, b, preferred_element_type=F32)


def nt(a, b):
    return lax.dot_general(a, b, (((1,), (1,)), ((), ())), preferred_element_type=F32)


def tn(a, b):
    return lax.dot_general(a, b, (((0,), (0,)), ((), ())), preferred_element_type=F32)


def iota(shape, axis):
    return lax.broadcasted_iota(jnp.int32, shape, axis)


def slots_and_gates(ids_ref, votes_ref, experts, capacity):
    rows = ids_ref.shape[1]
    ids = ids_ref[...].astype(F32).T.astype(jnp.int32)
    first, second = ids[:, 0:1], ids[:, 1:2]
    names = iota((rows, experts), 1)
    hot0 = (names == first).astype(F32)
    hot1 = (names == second).astype(F32)
    earlier = (iota((rows, rows), 0) > iota((rows, rows), 1)).astype(BF)
    before = nn(earlier, (hot0 + hot1).astype(BF))
    rank0 = jnp.sum(before * hot0, axis=1, keepdims=True).astype(jnp.int32)
    rank1 = jnp.sum(before * hot1, axis=1, keepdims=True).astype(jnp.int32)
    votes = votes_ref[...].astype(F32).T
    total = votes[:, 0:1] + votes[:, 1:2]
    slot0 = first * (2 * capacity) + rank0
    slot1 = second * (2 * capacity) + rank1
    return slot0, slot1, votes[:, 0:1] / total, votes[:, 1:2] / total


def pick(rows, factor, j):
    shape = (rows, rows * factor)
    return (iota(shape, 1) == iota(shape, 0) * factor + j).astype(BF)


def pack_kernel(w_gate, w_up, w_down, first, second, held, in_sem, out_sem):
    width = w_gate.shape[1]
    half = first.shape[0]
    loads = [pltpu.make_async_copy(src.at[0], held.at[pl.ds(m * width, width)], in_sem.at[m]) for m, src in enumerate((w_gate, w_up, w_down))]
    stores = [pltpu.make_async_copy(held.at[pl.ds(h * half, half)], dst, out_sem.at[h]) for h, dst in enumerate((first, second))]
    for copy in loads:
        copy.start()
    for copy in loads[:2]:
        copy.wait()
    stores[0].start()
    loads[2].wait()
    stores[1].start()
    for copy in stores:
        copy.wait()


def before_kernel(experts, capacity, tokens, cotangent, ids, votes, pool, norm, gain, send, scaled_out, notes):
    rows = ids.shape[1]
    factor = tokens.shape[0] // rows
    slot0, slot1, gate0, gate1 = slots_and_gates(ids, votes, experts, capacity)
    tok = tokens[...]
    cot = cotangent[...]
    short = None
    d_mix = None
    for j in range(factor):
        sel = pick(rows, factor, j)
        a = nn(sel, tok) * pool[j : j + 1, :]
        b = nn(sel, cot) * gain[j : j + 1, :]
        short = a if short is None else short + a
        d_mix = b if d_mix is None else d_mix + b
    inv = lax.rsqrt(jnp.mean(short * short, axis=1, keepdims=True) + 1e-06)
    scaled = short * inv
    scaled_out[...] = scaled
    lane = iota(notes.shape, 1)
    noted = inv
    for n, column in enumerate((slot0.astype(F32), slot1.astype(F32), gate0, gate1)):
        noted = jnp.where(lane == n + 1, column, noted)
    notes[...] = noted
    values = jnp.concatenate(
        [
            (scaled * norm[...]).astype(BF),
            (gate0 * d_mix).astype(BF),
            (gate1 * d_mix).astype(BF),
        ],
        axis=0,
    )
    place = iota((rows, send.shape[0]), 1)
    spread = jnp.concatenate(
        [
            jnp.where((place == slot0) | (place == slot1), 1.0, 0.0).astype(BF),
            jnp.where(place == slot0 + capacity, 1.0, 0.0).astype(BF),
            jnp.where(place == slot1 + capacity, 1.0, 0.0).astype(BF),
        ],
        axis=0,
    )
    send[...] = tn(spread, values).astype(BF)


def split_matrix(rows, capacity):
    half = rows // 2
    r = iota((rows, rows), 0)
    c = iota((rows, rows), 1)
    kind = (r >= half).astype(jnp.int32)
    within = r - kind * half
    sender = ((within.astype(F32) + 0.5) * (1.0 / capacity)).astype(jnp.int32)
    source = within + (sender + kind) * capacity
    return (c == source).astype(BF)


def experts_kernel(capacity, group, cols, arrived, *refs):
    halves, refs = refs[:16], refs[16:]
    back, packed, left_out, mixed, w, xs, gs, acts, lefts, in_sem, w_sem, out_sem, back_sem = refs
    half = group // 2
    groups = arrived.shape[0] // group
    pieces, three, model = w.shape
    width = three // 3
    full = pieces * width
    parts = 4
    step = parts * width
    loads = [
        pltpu.make_async_copy(arrived.at[pl.ds(i * group, group)], mixed.at[pl.ds(i * group, group)], in_sem.at[i])
        for i in range(groups)
    ]
    held = [
        pltpu.make_async_copy(src, w.at[i // 2, pl.ds((i % 2) * (three // 2), three // 2)], w_sem.at[i]) for i, src in enumerate(halves)
    ]
    chunk = 2 * parts
    for copy in loads + held[:chunk]:
        copy.start()
    sel = split_matrix(group, capacity)
    for i in range(groups):
        loads[i].wait()
        if i == 1:
            for copy in held[chunk : 2 * chunk]:
                copy.start()
        both = nn(sel, mixed[i * group : (i + 1) * group, :]).astype(BF)
        xs[i * half : (i + 1) * half, :] = both[:half]
        gs[i * half : (i + 1) * half, :] = both[half:]
    outs = [pltpu.make_async_copy(src, packed.at[:, pl.ds(i * model, model)], out_sem.at[i]) for i, src in enumerate((xs, gs))]
    for c in range(pieces // parts):
        for copy in held[c * chunk : (c + 1) * chunk]:
            copy.wait()
        if c == 0:
            for copy in outs:
                copy.start()
        for copy in held[(c + 2) * chunk : (c + 3) * chunk]:
            copy.start()
        mine = slice(c * parts, (c + 1) * parts)
        x = xs[...]
        pre_gate = nt(x, w[mine, 0:width].reshape(step, model))
        pre_up = nt(x, w[mine, width : 2 * width].reshape(step, model))
        d_hidden = nt(gs[...], w[mine, 2 * width :].reshape(step, model))
        sig = jax.nn.sigmoid(pre_gate)
        active = pre_gate * sig
        hidden = active * pre_up
        d_gate = d_hidden * pre_up * sig * (1.0 + pre_gate * (1.0 - sig))
        d_up = d_hidden * active
        at = slice(c * step, (c + 1) * step)
        for m, part in enumerate((d_gate, d_up, hidden)):
            rounded = part.astype(BF)
            acts[m, :, at] = rounded
            if 2 * c < pieces // parts:
                lefts[m, at, :] = rounded.T
    mine = full // 2
    last = [pltpu.make_async_copy(lefts, left_out, out_sem.at[2])]
    for m in range(3):
        theirs = packed.at[:, pl.ds(2 * model + m * mine, mine)]
        last.append(pltpu.make_async_copy(acts.at[m, :, pl.ds(mine, mine)], theirs, out_sem.at[3 + m]))
    for copy in last:
        copy.start()
    outs += last
    for n in range(model // cols):
        at = slice(n * cols, (n + 1) * cols)
        y = nn(acts[2], w[:, 2 * width :, at].reshape(full, cols)).astype(BF)
        dx = nn(acts[0], w[:, 0:width, at].reshape(full, cols)) + nn(acts[1], w[:, width : 2 * width, at].reshape(full, cols))
        dx = dx.astype(BF)
        for i in range(groups):
            both = jnp.concatenate([y[i * half : (i + 1) * half], dx[i * half : (i + 1) * half]], axis=0)
            mixed[i * group : (i + 1) * group, at] = tn(sel, both).astype(BF)
        copy = pltpu.make_async_copy(mixed.at[:, pl.ds(n * cols, cols)], back.at[:, pl.ds(n * cols, cols)], back_sem.at[n])
        copy.start()
        outs.append(copy)
    for copy in outs:
        copy.wait()


def experts_call(arrived, halves, capacity):
    slots, width = arrived.shape
    three = 2 * halves[0].shape[0]
    pieces = len(halves) // 2
    full = pieces * three // 3
    rows = slots // 2
    group = 16 * capacity
    cols = width // 2
    hbm = pl.BlockSpec(memory_space=pl.ANY)
    return pl.pallas_call(
        functools.partial(experts_kernel, capacity, group, cols),
        in_specs=[hbm] * (1 + len(halves)),
        out_specs=[hbm] * 3,
        out_shape=(
            jax.ShapeDtypeStruct((slots, width), BF),
            jax.ShapeDtypeStruct((rows, 2 * width + 3 * full // 2), BF),
            jax.ShapeDtypeStruct((3, full // 2, rows), BF),
        ),
        scratch_shapes=[
            pltpu.VMEM((slots, width), BF),
            pltpu.VMEM((pieces, three, width), BF),
            pltpu.VMEM((rows, width), BF),
            pltpu.VMEM((rows, width), BF),
            pltpu.VMEM((3, rows, full), BF),
            pltpu.VMEM((3, full // 2, rows), BF),
            pltpu.SemaphoreType.DMA((slots // group,)),
            pltpu.SemaphoreType.DMA((len(halves),)),
            pltpu.SemaphoreType.DMA((6,)),
            pltpu.SemaphoreType.DMA((width // cols,)),
        ],
        compiler_params=pltpu.CompilerParams(vmem_limit_bytes=EXPERTS_LIMIT),
        cost_estimate=pl.CostEstimate(flops=12 * rows * full * width, bytes_accessed=8 * slots * width, transcendentals=rows * full),
        name="experts",
    )(arrived, *halves)


def sums_kernel(jobs, packed_a, left_a, packed_b, d0, d1, d2, d3, x, g, left, acts, p, in_sem, out_sem):
    rows = left_a.shape[2]
    model = x.shape[1]
    mine = left.shape[1]
    _, three, cols = p.shape
    width = three // 3
    def load(src, dst, n):
        return pltpu.make_async_copy(src, dst, in_sem.at[n])

    lefts = load(left_a, left.at[:, :, pl.ds(0, rows)], 0)
    theirs = [load(packed_b.at[:, pl.ds(2 * model + m * mine, mine)], acts.at[m], 1 + m) for m in range(3)]
    sides = []
    for j, side in enumerate((x, g)):
        for i, src in enumerate((packed_a, packed_b)):
            sides.append(load(src.at[:, pl.ds(j * model, model)], side.at[pl.ds(i * rows, rows)], 4 + 2 * j + i))
    for copy in theirs + [lefts] + sides:
        copy.start()
    for m in range(3):
        theirs[m].wait()
        left[m, :, rows:] = acts[m].T
    lefts.wait()
    outs = []
    dsts = (d0, d1, d2, d3)
    for m, right in enumerate((x, x, g)):
        for copy in (sides[0:2], [], sides[2:4])[m]:
            copy.wait()
        for i, (half, pair) in enumerate(jobs):
            lhs = jnp.concatenate([left[m, k * width : (k + 1) * width, :] for k in pair], axis=0)
            found = nn(lhs, right[:, half * cols : (half + 1) * cols]).astype(BF)
            for j in range(2):
                p[2 * i + j, m * width : (m + 1) * width, :] = found[j * width : (j + 1) * width]
                at = pl.ds(m * width, width)
                copy = pltpu.make_async_copy(p.at[2 * i + j, at], dsts[2 * i + j].at[at], out_sem.at[m, 2 * i + j])
                copy.start()
                outs.append(copy)
    for copy in outs:
        copy.wait()


def sums_call(packed, left, theirs, pieces, jobs, name):
    _, mine, rows = left.shape
    width = (packed.shape[1] - 3 * mine) // 2
    three = 3 * mine // pieces
    hbm = pl.BlockSpec(memory_space=pl.ANY)
    return pl.pallas_call(
        functools.partial(sums_kernel, jobs),
        in_specs=[hbm] * 3,
        out_specs=[hbm] * 4,
        out_shape=(jax.ShapeDtypeStruct((three, width // 2), BF),) * 4,
        scratch_shapes=[
            pltpu.VMEM((2 * rows, width), BF),
            pltpu.VMEM((2 * rows, width), BF),
            pltpu.VMEM((3, mine, 2 * rows), BF),
            pltpu.VMEM((3, rows, mine), BF),
            pltpu.VMEM((4, three, width // 2), BF),
            pltpu.SemaphoreType.DMA((8,)),
            pltpu.SemaphoreType.DMA((3, 4)),
        ],
        compiler_params=pltpu.CompilerParams(vmem_limit_bytes=SUMS_LIMIT),
        cost_estimate=pl.CostEstimate(flops=6 * rows * mine * width, bytes_accessed=16 * rows * width, transcendentals=0),
        name=name,
    )(packed, left, theirs)


def grads_kernel(q0a, q0b, q1a, q1b, q2a, q2b, o_gate, o_up, o_down, q, total, q_sem, o_sem):
    cols = q.shape[2] // 2
    loads = [
        pltpu.make_async_copy(src, q.at[k // 2, :, pl.ds((k % 2) * cols, cols)], q_sem.at[k]) for k, src in enumerate((q0a, q0b, q1a, q1b, q2a, q2b))
    ]
    for copy in loads:
        copy.start()
    for copy in loads:
        copy.wait()
    stores = []
    width = total.shape[1]
    for m, dst in enumerate((o_gate, o_up, o_down)):
        at = slice(m * width, (m + 1) * width)
        terms = [q[k, at].astype(F32) for k in range(3)]
        total[m] = terms[0] + terms[1] + terms[2]
        copy = pltpu.make_async_copy(total.at[m], dst.at[0], o_sem.at[m])
        copy.start()
        stores.append(copy)
    for copy in stores:
        copy.wait()


def after_kernel(capacity, table, scaled_in, notes, pool, norm, gain, out, grad, out_buf, grad_buf, sem):
    rows, model = scaled_in.shape
    factor = out.shape[0] // rows
    inv, gate0, gate1 = notes[:, 0:1], notes[:, 3:4], notes[:, 4:5]
    slot0, slot1 = notes[:, 1:2].astype(jnp.int32), notes[:, 2:3].astype(jnp.int32)
    place = iota((rows, table.shape[0]), 1)
    grad0, grad1 = slot0 + capacity, slot1 + capacity
    sel = jnp.concatenate(
        [
            jnp.where(place == slot0, 1.0, 0.0).astype(BF),
            jnp.where(place == slot1, 1.0, 0.0).astype(BF),
            jnp.where((place == grad0) | (place == grad1), 1.0, 0.0).astype(BF),
        ],
        axis=0,
    )
    mix = jnp.concatenate([pick(rows, factor, j) for j in range(factor)], axis=0)
    found = nn(sel, table[...])
    mixture = gate0 * found[:rows] + gate1 * found[rows : 2 * rows]
    outs = jnp.concatenate([(gain[j : j + 1, :] * mixture).astype(BF) for j in range(factor)], axis=0)
    out_buf[...] = tn(mix, outs).astype(BF)
    first = pltpu.make_async_copy(out_buf, out, sem.at[0])
    first.start()
    d_scaled = found[2 * rows :] * norm[...]
    scaled = scaled_in[...]
    d_short = inv * (d_scaled - scaled * jnp.mean(d_scaled * scaled, axis=1, keepdims=True))
    grads = jnp.concatenate([(pool[j : j + 1, :] * d_short).astype(BF) for j in range(factor)], axis=0)
    half = model // 2
    copies = [first]
    for n in range(2):
        at = slice(n * half, (n + 1) * half)
        grad_buf[:, at] = tn(mix, grads[:, at]).astype(BF)
        copy = pltpu.make_async_copy(grad_buf.at[:, pl.ds(n * half, half)], grad.at[:, pl.ds(n * half, half)], sem.at[1 + n])
        copy.start()
        copies.append(copy)
    for copy in copies:
        copy.wait()


def shards(
    tokens,
    cotangent,
    expert_ids,
    votes,
    pool_weight,
    norm_gain,
    up_gain,
    gate_weight,
    up_weight,
    down_weight,
):
    ring = lax.axis_size("y")
    experts = lax.axis_size("z") * lax.axis_size("x")
    rows, top = expert_ids.shape
    width = tokens.shape[1]
    hidden = gate_weight.shape[1]
    capacity = 2 * rows * top // experts
    slots = 2 * experts * capacity
    params = pltpu.CompilerParams(vmem_limit_bytes=EDGE_LIMIT)
    vmem = pl.BlockSpec(memory_space=pltpu.VMEM)
    hbm = pl.BlockSpec(memory_space=pl.ANY)
    norm = norm_gain[None]
    ids, counts = expert_ids.T, votes.T

    def move(a, k):
        return lax.ppermute(a, "y", [(i, (i + k) % ring) for i in range(ring)])

    def swap(a):
        return lax.ppermute(a, "core", [(0, 1), (1, 0)])

    def exchange(a):
        return lax.all_to_all(a, ("z", "x"), split_axis=0, concat_axis=0, tiled=True)

    up, down = 1, ring - 1
    h0, h1 = pl.pallas_call(
        pack_kernel,
        in_specs=[hbm] * 3,
        out_specs=[hbm] * 2,
        out_shape=(jax.ShapeDtypeStruct((3 * hidden // 2, width), BF),) * 2,
        scratch_shapes=[pltpu.VMEM((3 * hidden, width), BF), pltpu.SemaphoreType.DMA((3,)), pltpu.SemaphoreType.DMA((2,))],
        compiler_params=params,
        name="pack",
    )(gate_weight, up_weight, down_weight)
    u0, d1 = move(h0, up), move(h1, down)
    t0, t1 = move(u0, up), move(d1, down)
    u1, d0 = move(h1, up), move(h0, down)
    halves = [h0, h1, u0, u1, t0, t1, d0, d1]
    halves = halves + [swap(a) for a in halves]

    send, scaled, notes = pl.pallas_call(
        functools.partial(before_kernel, experts, capacity),
        out_shape=(
            jax.ShapeDtypeStruct((slots, width), BF),
            jax.ShapeDtypeStruct((rows, width), F32),
            jax.ShapeDtypeStruct((rows, 128), F32),
        ),
        compiler_params=params,
        name="before",
    )(tokens, cotangent, ids, counts, pool_weight, norm, up_gain)

    arrived = exchange(send)
    back, packed, left = experts_call(arrived, halves, capacity)
    theirs = swap(packed)
    returned = exchange(back)
    p2a, p3a, p1b, p2b = sums_call(packed, left, theirs, ring, ((0, (2, 3)), (1, (1, 2))), "sums_far")
    p0a, p1a, p3b, p0b = sums_call(packed, left, theirs, ring, ((0, (0, 1)), (1, (3, 0))), "sums_near")
    r1b, r3a = move(p1b, down), move(p3a, up)
    r1a = move(p1a + move(p2a, down), down)
    r3b = move(p3b + move(p2b, up), up)
    parts = (p0a, p0b, r1a, r1b, r3a, r3b)

    held = jax.ShapeDtypeStruct((1, hidden, width), F32)
    grads = pl.pallas_call(
        grads_kernel,
        in_specs=[hbm] * 6,
        out_specs=[hbm] * 3,
        out_shape=(held, held, held),
        scratch_shapes=[
            pltpu.VMEM((3, 3 * hidden, width), BF),
            pltpu.VMEM((3, hidden, width), F32),
            pltpu.SemaphoreType.DMA((6,)),
            pltpu.SemaphoreType.DMA((3,)),
        ],
        compiler_params=params,
        name="grads",
    )(*parts)

    shape = jax.ShapeDtypeStruct(tokens.shape, BF)
    layer_out, tokens_grad = pl.pallas_call(
        functools.partial(after_kernel, capacity),
        in_specs=[vmem] * 6,
        out_specs=[hbm] * 2,
        out_shape=(shape, shape),
        scratch_shapes=[pltpu.VMEM(tokens.shape, BF), pltpu.VMEM(tokens.shape, BF), pltpu.SemaphoreType.DMA((3,))],
        compiler_params=pltpu.CompilerParams(vmem_limit_bytes=AFTER_LIMIT),
        name="after",
    )(returned, scaled, notes, pool_weight, norm, up_gain)
    return (layer_out, tokens_grad, *grads)


def solution(mesh):
    sizes = (mesh.shape["dp"] // 2, 2, mesh.shape["expert"] // 4, 4)
    mesh = jax.sharding.Mesh(mesh.devices.reshape(sizes), ("y", "core", "z", "x"))
    rows = P(("y", "core", "z", "x"), None)
    held = P(("z", "x"), ("y", "core"), None)
    return jax.shard_map(
        shards,
        mesh=mesh,
        in_specs=(rows, rows, rows, rows, P(), P(), P(), held, held, held),
        out_specs=(rows, rows, held, held, held),
        check_vma=False,
    )
```

```python
import functools

import jax
import jax.numpy as jnp
from jax import lax
from jax.experimental import pallas as pl
from jax.experimental.pallas import tpu as pltpu
from jax.sharding import PartitionSpec as P

BF = jnp.bfloat16
F32 = jnp.float32
MIB = 1024 * 1024
EDGE_LIMIT = 60 * MIB
AFTER_LIMIT = 52 * MIB
EXPERTS_LIMIT = 51 * MIB
SUMS_LIMIT = 60 * MIB


def nn(a, b):
    return jnp.dot(a, b, preferred_element_type=F32)


def nt(a, b):
    return lax.dot_general(a, b, (((1,), (1,)), ((), ())), preferred_element_type=F32)


def tn(a, b):
    return lax.dot_general(a, b, (((0,), (0,)), ((), ())), preferred_element_type=F32)


def iota(shape, axis):
    return lax.broadcasted_iota(jnp.int32, shape, axis)


def slots_and_gates(ids_ref, votes_ref, experts, capacity):
    rows = ids_ref.shape[1]
    ids = ids_ref[...].astype(F32).T.astype(jnp.int32)
    first, second = ids[:, 0:1], ids[:, 1:2]
    names = iota((rows, experts), 1)
    hot0 = (names == first).astype(F32)
    hot1 = (names == second).astype(F32)
    earlier = (iota((rows, rows), 0) > iota((rows, rows), 1)).astype(BF)
    before = nn(earlier, (hot0 + hot1).astype(BF))
    rank0 = jnp.sum(before * hot0, axis=1, keepdims=True).astype(jnp.int32)
    rank1 = jnp.sum(before * hot1, axis=1, keepdims=True).astype(jnp.int32)
    votes = votes_ref[...].astype(F32).T
    total = votes[:, 0:1] + votes[:, 1:2]
    slot0 = first * (2 * capacity) + rank0
    slot1 = second * (2 * capacity) + rank1
    return slot0, slot1, votes[:, 0:1] / total, votes[:, 1:2] / total


def pick(rows, factor, j):
    shape = (rows, rows * factor)
    return (iota(shape, 1) == iota(shape, 0) * factor + j).astype(BF)


def pack_kernel(w_gate, w_up, w_down, first, second, held, in_sem, out_sem):
    width = w_gate.shape[1]
    half = first.shape[0]
    loads = [pltpu.make_async_copy(src.at[0], held.at[pl.ds(m * width, width)], in_sem.at[m]) for m, src in enumerate((w_gate, w_up, w_down))]
    stores = [pltpu.make_async_copy(held.at[pl.ds(h * half, half)], dst, out_sem.at[h]) for h, dst in enumerate((first, second))]
    for copy in loads:
        copy.start()
    for copy in loads[:2]:
        copy.wait()
    stores[0].start()
    loads[2].wait()
    stores[1].start()
    for copy in stores:
        copy.wait()


def before_kernel(experts, capacity, tokens, cotangent, ids, votes, pool, norm, gain, send, scaled_out, notes):
    rows = ids.shape[1]
    factor = tokens.shape[0] // rows
    slot0, slot1, gate0, gate1 = slots_and_gates(ids, votes, experts, capacity)
    band = rows // 3
    sel = jnp.concatenate([pick(band, factor, j) for j in range(factor)], axis=0)
    shorts, mixes = [], []
    for i in range(3):
        at = slice(i * band * factor, (i + 1) * band * factor)
        tok, cot = nn(sel, tokens[at, :]), nn(sel, cotangent[at, :])
        short = d_mix = None
        for j in range(factor):
            a = tok[j * band : (j + 1) * band] * pool[j : j + 1, :]
            b = cot[j * band : (j + 1) * band] * gain[j : j + 1, :]
            short = a if short is None else short + a
            d_mix = b if d_mix is None else d_mix + b
        shorts.append(short)
        mixes.append(d_mix)
    short = jnp.concatenate(shorts, axis=0)
    d_mix = jnp.concatenate(mixes, axis=0)
    inv = lax.rsqrt(jnp.mean(short * short, axis=1, keepdims=True) + 1e-06)
    scaled = short * inv
    scaled_out[...] = scaled
    lane = iota(notes.shape, 1)
    noted = inv
    for n, column in enumerate((slot0.astype(F32), slot1.astype(F32), gate0, gate1)):
        noted = jnp.where(lane == n + 1, column, noted)
    notes[...] = noted
    values = jnp.concatenate(
        [
            (scaled * norm[...]).astype(BF),
            (gate0 * d_mix).astype(BF),
            (gate1 * d_mix).astype(BF),
        ],
        axis=0,
    )
    place = iota((rows, send.shape[0]), 1)
    spread = jnp.concatenate(
        [
            jnp.where((place == slot0) | (place == slot1), 1.0, 0.0).astype(BF),
            jnp.where(place == slot0 + capacity, 1.0, 0.0).astype(BF),
            jnp.where(place == slot1 + capacity, 1.0, 0.0).astype(BF),
        ],
        axis=0,
    )
    send[...] = tn(spread, values).astype(BF)


def split_matrix(rows, capacity):
    half = rows // 2
    r = iota((rows, rows), 0)
    c = iota((rows, rows), 1)
    kind = (r >= half).astype(jnp.int32)
    within = r - kind * half
    sender = ((within.astype(F32) + 0.5) * (1.0 / capacity)).astype(jnp.int32)
    source = within + (sender + kind) * capacity
    return (c == source).astype(BF)


def experts_kernel(capacity, group, cols, arrived, *refs):
    halves, refs = refs[:16], refs[16:]
    back, packed, left_out, mixed, w, xs, gs, acts, lefts, in_sem, w_sem, out_sem, back_sem = refs
    half = group // 2
    groups = arrived.shape[0] // group
    pieces, three, model = w.shape
    width = three // 3
    full = pieces * width
    parts = 4
    step = parts * width
    loads = [
        pltpu.make_async_copy(arrived.at[pl.ds(i * group, group)], mixed.at[pl.ds(i * group, group)], in_sem.at[i])
        for i in range(groups)
    ]
    held = [
        pltpu.make_async_copy(src, w.at[i // 2, pl.ds((i % 2) * (three // 2), three // 2)], w_sem.at[i]) for i, src in enumerate(halves)
    ]
    chunk = 2 * parts
    for copy in loads + held[:chunk]:
        copy.start()
    sel = split_matrix(group, capacity)
    for i in range(groups):
        loads[i].wait()
        if i == 1:
            for copy in held[chunk : 2 * chunk]:
                copy.start()
        both = nn(sel, mixed[i * group : (i + 1) * group, :]).astype(BF)
        xs[i * half : (i + 1) * half, :] = both[:half]
        gs[i * half : (i + 1) * half, :] = both[half:]
    outs = [pltpu.make_async_copy(src, packed.at[:, pl.ds(i * model, model)], out_sem.at[i]) for i, src in enumerate((xs, gs))]
    for c in range(pieces // parts):
        for copy in held[c * chunk : (c + 1) * chunk]:
            copy.wait()
        if c == 0:
            for copy in outs:
                copy.start()
        for copy in held[(c + 2) * chunk : (c + 3) * chunk]:
            copy.start()
        mine = slice(c * parts, (c + 1) * parts)
        x = xs[...]
        pre_gate = nt(x, w[mine, 0:width].reshape(step, model))
        pre_up = nt(x, w[mine, width : 2 * width].reshape(step, model))
        d_hidden = nt(gs[...], w[mine, 2 * width :].reshape(step, model))
        sig = jax.nn.sigmoid(pre_gate)
        active = pre_gate * sig
        hidden = active * pre_up
        d_gate = d_hidden * pre_up * sig * (1.0 + pre_gate * (1.0 - sig))
        d_up = d_hidden * active
        at = slice(c * step, (c + 1) * step)
        for m, part in enumerate((d_gate, d_up, hidden)):
            rounded = part.astype(BF)
            acts[m, :, at] = rounded
            if 2 * c < pieces // parts:
                lefts[m, at, :] = rounded.T
    mine = full // 2
    last = [pltpu.make_async_copy(lefts, left_out, out_sem.at[2])]
    for m in range(3):
        theirs = packed.at[:, pl.ds(2 * model + m * mine, mine)]
        last.append(pltpu.make_async_copy(acts.at[m, :, pl.ds(mine, mine)], theirs, out_sem.at[3 + m]))
    for copy in last:
        copy.start()
    outs += last
    for n in range(model // cols):
        at = slice(n * cols, (n + 1) * cols)
        y = nn(acts[2], w[:, 2 * width :, at].reshape(full, cols)).astype(BF)
        dx = nn(acts[0], w[:, 0:width, at].reshape(full, cols)) + nn(acts[1], w[:, width : 2 * width, at].reshape(full, cols))
        dx = dx.astype(BF)
        for i in range(groups):
            both = jnp.concatenate([y[i * half : (i + 1) * half], dx[i * half : (i + 1) * half]], axis=0)
            mixed[i * group : (i + 1) * group, at] = tn(sel, both).astype(BF)
        copy = pltpu.make_async_copy(mixed.at[:, pl.ds(n * cols, cols)], back.at[:, pl.ds(n * cols, cols)], back_sem.at[n])
        copy.start()
        outs.append(copy)
    for copy in outs:
        copy.wait()


def experts_call(arrived, halves, capacity):
    slots, width = arrived.shape
    three = 2 * halves[0].shape[0]
    pieces = len(halves) // 2
    full = pieces * three // 3
    rows = slots // 2
    group = 16 * capacity
    cols = width // 2
    hbm = pl.BlockSpec(memory_space=pl.ANY)
    return pl.pallas_call(
        functools.partial(experts_kernel, capacity, group, cols),
        in_specs=[hbm] * (1 + len(halves)),
        out_specs=[hbm] * 3,
        out_shape=(
            jax.ShapeDtypeStruct((slots, width), BF),
            jax.ShapeDtypeStruct((rows, 2 * width + 3 * full // 2), BF),
            jax.ShapeDtypeStruct((3, full // 2, rows), BF),
        ),
        scratch_shapes=[
            pltpu.VMEM((slots, width), BF),
            pltpu.VMEM((pieces, three, width), BF),
            pltpu.VMEM((rows, width), BF),
            pltpu.VMEM((rows, width), BF),
            pltpu.VMEM((3, rows, full), BF),
            pltpu.VMEM((3, full // 2, rows), BF),
            pltpu.SemaphoreType.DMA((slots // group,)),
            pltpu.SemaphoreType.DMA((len(halves),)),
            pltpu.SemaphoreType.DMA((6,)),
            pltpu.SemaphoreType.DMA((width // cols,)),
        ],
        compiler_params=pltpu.CompilerParams(vmem_limit_bytes=EXPERTS_LIMIT),
        cost_estimate=pl.CostEstimate(flops=12 * rows * full * width, bytes_accessed=8 * slots * width, transcendentals=rows * full),
        name="experts",
    )(arrived, *halves)


def sums_kernel(jobs, packed_a, left_a, packed_b, d0, d1, d2, d3, x, g, left, acts, p, in_sem, out_sem):
    rows = left_a.shape[2]
    model = x.shape[1]
    mine = left.shape[1]
    _, three, cols = p.shape
    width = three // 3
    def load(src, dst, n):
        return pltpu.make_async_copy(src, dst, in_sem.at[n])

    lefts = load(left_a, left.at[:, :, pl.ds(0, rows)], 0)
    theirs = [load(packed_b.at[:, pl.ds(2 * model + m * mine, mine)], acts.at[m], 1 + m) for m in range(3)]
    sides = []
    for j, side in enumerate((x, g)):
        for i, src in enumerate((packed_a, packed_b)):
            sides.append(load(src.at[:, pl.ds(j * model, model)], side.at[pl.ds(i * rows, rows)], 4 + 2 * j + i))
    for copy in theirs + [lefts] + sides:
        copy.start()
    for m in range(3):
        theirs[m].wait()
        left[m, :, rows:] = acts[m].T
    lefts.wait()
    outs = []
    dsts = (d0, d1, d2, d3)
    for m, right in enumerate((x, x, g)):
        for copy in (sides[0:2], [], sides[2:4])[m]:
            copy.wait()
        for i, (half, pair) in enumerate(jobs):
            lhs = jnp.concatenate([left[m, k * width : (k + 1) * width, :] for k in pair], axis=0)
            found = nn(lhs, right[:, half * cols : (half + 1) * cols]).astype(BF)
            for j in range(2):
                p[2 * i + j, m * width : (m + 1) * width, :] = found[j * width : (j + 1) * width]
                at = pl.ds(m * width, width)
                copy = pltpu.make_async_copy(p.at[2 * i + j, at], dsts[2 * i + j].at[at], out_sem.at[m, 2 * i + j])
                copy.start()
                outs.append(copy)
    for copy in outs:
        copy.wait()


def sums_call(packed, left, theirs, pieces, jobs, name):
    _, mine, rows = left.shape
    width = (packed.shape[1] - 3 * mine) // 2
    three = 3 * mine // pieces
    hbm = pl.BlockSpec(memory_space=pl.ANY)
    return pl.pallas_call(
        functools.partial(sums_kernel, jobs),
        in_specs=[hbm] * 3,
        out_specs=[hbm] * 4,
        out_shape=(jax.ShapeDtypeStruct((three, width // 2), BF),) * 4,
        scratch_shapes=[
            pltpu.VMEM((2 * rows, width), BF),
            pltpu.VMEM((2 * rows, width), BF),
            pltpu.VMEM((3, mine, 2 * rows), BF),
            pltpu.VMEM((3, rows, mine), BF),
            pltpu.VMEM((4, three, width // 2), BF),
            pltpu.SemaphoreType.DMA((8,)),
            pltpu.SemaphoreType.DMA((3, 4)),
        ],
        compiler_params=pltpu.CompilerParams(vmem_limit_bytes=SUMS_LIMIT),
        cost_estimate=pl.CostEstimate(flops=6 * rows * mine * width, bytes_accessed=16 * rows * width, transcendentals=0),
        name=name,
    )(packed, left, theirs)


def grads_kernel(q0a, q0b, q1a, q1b, q2a, q2b, o_gate, o_up, o_down, q, total, q_sem, o_sem):
    cols = q.shape[2] // 2
    loads = [
        pltpu.make_async_copy(src, q.at[k // 2, :, pl.ds((k % 2) * cols, cols)], q_sem.at[k]) for k, src in enumerate((q0a, q0b, q1a, q1b, q2a, q2b))
    ]
    for copy in loads:
        copy.start()
    for copy in loads:
        copy.wait()
    stores = []
    width = total.shape[1]
    for m, dst in enumerate((o_gate, o_up, o_down)):
        at = slice(m * width, (m + 1) * width)
        terms = [q[k, at].astype(F32) for k in range(3)]
        total[m] = terms[0] + terms[1] + terms[2]
        copy = pltpu.make_async_copy(total.at[m], dst.at[0], o_sem.at[m])
        copy.start()
        stores.append(copy)
    for copy in stores:
        copy.wait()


def after_kernel(capacity, table, scaled_in, notes, pool, norm, gain, out, grad, out_buf, grad_buf, sem):
    rows, model = scaled_in.shape
    factor = out.shape[0] // rows
    inv, gate0, gate1 = notes[:, 0:1], notes[:, 3:4], notes[:, 4:5]
    slot0, slot1 = notes[:, 1:2].astype(jnp.int32), notes[:, 2:3].astype(jnp.int32)
    place = iota((rows, table.shape[0]), 1)
    grad0, grad1 = slot0 + capacity, slot1 + capacity
    sel = jnp.concatenate(
        [
            jnp.where(place == slot0, 1.0, 0.0).astype(BF),
            jnp.where(place == slot1, 1.0, 0.0).astype(BF),
            jnp.where((place == grad0) | (place == grad1), 1.0, 0.0).astype(BF),
        ],
        axis=0,
    )
    band = rows // 3
    mix = jnp.concatenate([pick(band, factor, j) for j in range(factor)], axis=0)
    copies = []

    def store(values, scale, buf, dst, first):
        for i in range(3):
            part = values[i * band : (i + 1) * band]
            blocks = jnp.concatenate([(scale[j : j + 1, :] * part).astype(BF) for j in range(factor)], axis=0)
            at = slice(i * band * factor, (i + 1) * band * factor)
            buf[at, :] = tn(mix, blocks).astype(BF)
            span = pl.ds(i * band * factor, band * factor)
            copy = pltpu.make_async_copy(buf.at[span], dst.at[span], sem.at[first + i])
            copy.start()
            copies.append(copy)

    found = nn(sel, table[...])
    mixture = gate0 * found[:rows] + gate1 * found[rows : 2 * rows]
    store(mixture, gain, out_buf, out, 0)
    d_scaled = found[2 * rows :] * norm[...]
    scaled = scaled_in[...]
    d_short = inv * (d_scaled - scaled * jnp.mean(d_scaled * scaled, axis=1, keepdims=True))
    store(d_short, pool, grad_buf, grad, 3)
    for copy in copies:
        copy.wait()


def shards(
    tokens,
    cotangent,
    expert_ids,
    votes,
    pool_weight,
    norm_gain,
    up_gain,
    gate_weight,
    up_weight,
    down_weight,
):
    ring = lax.axis_size("y")
    experts = lax.axis_size("z") * lax.axis_size("x")
    rows, top = expert_ids.shape
    width = tokens.shape[1]
    hidden = gate_weight.shape[1]
    capacity = 2 * rows * top // experts
    slots = 2 * experts * capacity
    params = pltpu.CompilerParams(vmem_limit_bytes=EDGE_LIMIT)
    vmem = pl.BlockSpec(memory_space=pltpu.VMEM)
    hbm = pl.BlockSpec(memory_space=pl.ANY)
    norm = norm_gain[None]
    ids, counts = expert_ids.T, votes.T

    def move(a, k):
        return lax.ppermute(a, "y", [(i, (i + k) % ring) for i in range(ring)])

    def swap(a):
        return lax.ppermute(a, "core", [(0, 1), (1, 0)])

    def exchange(a):
        return lax.all_to_all(a, ("z", "x"), split_axis=0, concat_axis=0, tiled=True)

    up, down = 1, ring - 1
    h0, h1 = pl.pallas_call(
        pack_kernel,
        in_specs=[hbm] * 3,
        out_specs=[hbm] * 2,
        out_shape=(jax.ShapeDtypeStruct((3 * hidden // 2, width), BF),) * 2,
        scratch_shapes=[pltpu.VMEM((3 * hidden, width), BF), pltpu.SemaphoreType.DMA((3,)), pltpu.SemaphoreType.DMA((2,))],
        compiler_params=params,
        name="pack",
    )(gate_weight, up_weight, down_weight)
    u0, d1 = move(h0, up), move(h1, down)
    t0, t1 = move(u0, up), move(d1, down)
    u1, d0 = move(h1, up), move(h0, down)
    halves = [h0, h1, u0, u1, t0, t1, d0, d1]
    least = jnp.asarray(jnp.finfo(BF).min, BF)
    halves = [jnp.maximum(h0, least), jnp.maximum(h1, least), *halves[2:]] + [swap(a) for a in halves]

    send, scaled, notes = pl.pallas_call(
        functools.partial(before_kernel, experts, capacity),
        out_shape=(
            jax.ShapeDtypeStruct((slots, width), BF),
            jax.ShapeDtypeStruct((rows, width), F32),
            jax.ShapeDtypeStruct((rows, 128), F32),
        ),
        compiler_params=params,
        name="before",
    )(tokens, cotangent, ids, counts, pool_weight, norm, up_gain)

    arrived = exchange(send)
    back, packed, left = experts_call(arrived, halves, capacity)
    theirs = swap(packed)
    returned = exchange(back)
    p2a, p3a, p1b, p2b = sums_call(packed, left, theirs, ring, ((0, (2, 3)), (1, (1, 2))), "sums_far")
    p0a, p1a, p3b, p0b = sums_call(packed, left, theirs, ring, ((0, (0, 1)), (1, (3, 0))), "sums_near")
    r1b, r3a = move(p1b, down), move(p3a, up)
    r1a = move(p1a + move(p2a, down), down)
    r3b = move(p3b + move(p2b, up), up)
    parts = (p0a, p0b, r1a, r1b, r3a, r3b)

    held = jax.ShapeDtypeStruct((1, hidden, width), F32)
    grads = pl.pallas_call(
        grads_kernel,
        in_specs=[hbm] * 6,
        out_specs=[hbm] * 3,
        out_shape=(held, held, held),
        scratch_shapes=[
            pltpu.VMEM((3, 3 * hidden, width), BF),
            pltpu.VMEM((3, hidden, width), F32),
            pltpu.SemaphoreType.DMA((6,)),
            pltpu.SemaphoreType.DMA((3,)),
        ],
        compiler_params=params,
        name="grads",
    )(*parts)

    shape = jax.ShapeDtypeStruct(tokens.shape, BF)
    layer_out, tokens_grad = pl.pallas_call(
        functools.partial(after_kernel, capacity),
        in_specs=[vmem] * 6,
        out_specs=[hbm] * 2,
        out_shape=(shape, shape),
        scratch_shapes=[pltpu.VMEM(tokens.shape, BF), pltpu.VMEM(tokens.shape, BF), pltpu.SemaphoreType.DMA((6,))],
        compiler_params=pltpu.CompilerParams(vmem_limit_bytes=AFTER_LIMIT),
        name="after",
    )(returned, scaled, notes, pool_weight, norm, up_gain)
    return (layer_out, tokens_grad, *grads)


def solution(mesh):
    sizes = (mesh.shape["dp"] // 2, 2, mesh.shape["expert"] // 4, 4)
    mesh = jax.sharding.Mesh(mesh.devices.reshape(sizes), ("y", "core", "z", "x"))
    rows = P(("y", "core", "z", "x"), None)
    held = P(("z", "x"), ("y", "core"), None)
    return jax.shard_map(
        shards,
        mesh=mesh,
        in_specs=(rows, rows, rows, rows, P(), P(), P(), held, held, held),
        out_specs=(rows, rows, held, held, held),
        check_vma=False,
    )
```

```python
import functools

import jax
import jax.numpy as jnp
from jax import lax
from jax.experimental import pallas as pl
from jax.experimental.pallas import tpu as pltpu
from jax.sharding import PartitionSpec as P

BF = jnp.bfloat16
F32 = jnp.float32
MIB = 1024 * 1024
EDGE_LIMIT = 60 * MIB
AFTER_LIMIT = 52 * MIB
EXPERTS_LIMIT = 51 * MIB
SUMS_LIMIT = 60 * MIB


def nn(a, b):
    return jnp.dot(a, b, preferred_element_type=F32)


def nt(a, b):
    return lax.dot_general(a, b, (((1,), (1,)), ((), ())), preferred_element_type=F32)


def tn(a, b):
    return lax.dot_general(a, b, (((0,), (0,)), ((), ())), preferred_element_type=F32)


def iota(shape, axis):
    return lax.broadcasted_iota(jnp.int32, shape, axis)


def slots_and_gates(ids_ref, votes_ref, experts, capacity):
    rows = ids_ref.shape[1]
    ids = ids_ref[...].astype(F32).T.astype(jnp.int32)
    first, second = ids[:, 0:1], ids[:, 1:2]
    names = iota((rows, experts), 1)
    hot0 = (names == first).astype(F32)
    hot1 = (names == second).astype(F32)
    earlier = (iota((rows, rows), 0) > iota((rows, rows), 1)).astype(BF)
    before = nn(earlier, (hot0 + hot1).astype(BF))
    rank0 = jnp.sum(before * hot0, axis=1, keepdims=True).astype(jnp.int32)
    rank1 = jnp.sum(before * hot1, axis=1, keepdims=True).astype(jnp.int32)
    votes = votes_ref[...].astype(F32).T
    total = votes[:, 0:1] + votes[:, 1:2]
    slot0 = first * (2 * capacity) + rank0
    slot1 = second * (2 * capacity) + rank1
    return slot0, slot1, votes[:, 0:1] / total, votes[:, 1:2] / total


def pick(rows, factor, j):
    shape = (rows, rows * factor)
    return (iota(shape, 1) == iota(shape, 0) * factor + j).astype(BF)


def pack_kernel(w_gate, w_up, w_down, first, second, held, in_sem, out_sem):
    width = w_gate.shape[1]
    half = first.shape[0]
    loads = [pltpu.make_async_copy(src.at[0], held.at[pl.ds(m * width, width)], in_sem.at[m]) for m, src in enumerate((w_gate, w_up, w_down))]
    stores = [pltpu.make_async_copy(held.at[pl.ds(h * half, half)], dst, out_sem.at[h]) for h, dst in enumerate((first, second))]
    for copy in loads:
        copy.start()
    for copy in loads[:2]:
        copy.wait()
    stores[0].start()
    loads[2].wait()
    stores[1].start()
    for copy in stores:
        copy.wait()


def before_kernel(experts, capacity, tokens, cotangent, ids, votes, pool, norm, gain, send, scaled_out, notes):
    rows = ids.shape[1]
    factor = tokens.shape[0] // rows
    slot0, slot1, gate0, gate1 = slots_and_gates(ids, votes, experts, capacity)
    band = rows // 3
    sel = jnp.concatenate([pick(band, factor, j) for j in range(factor)], axis=0)
    shorts, mixes = [], []
    for i in range(3):
        at = slice(i * band * factor, (i + 1) * band * factor)
        tok, cot = nn(sel, tokens[at, :]), nn(sel, cotangent[at, :])
        short = d_mix = None
        for j in range(factor):
            a = tok[j * band : (j + 1) * band] * pool[j : j + 1, :]
            b = cot[j * band : (j + 1) * band] * gain[j : j + 1, :]
            short = a if short is None else short + a
            d_mix = b if d_mix is None else d_mix + b
        shorts.append(short)
        mixes.append(d_mix)
    short = jnp.concatenate(shorts, axis=0)
    d_mix = jnp.concatenate(mixes, axis=0)
    inv = lax.rsqrt(jnp.mean(short * short, axis=1, keepdims=True) + 1e-06)
    scaled = short * inv
    scaled_out[...] = scaled
    lane = iota(notes.shape, 1)
    noted = inv
    for n, column in enumerate((slot0.astype(F32), slot1.astype(F32), gate0, gate1)):
        noted = jnp.where(lane == n + 1, column, noted)
    notes[...] = noted
    values = jnp.concatenate([(scaled * norm[...]).astype(BF), d_mix.astype(BF)], axis=0)
    place = iota((rows, send.shape[0]), 1)
    weighed = jnp.where(place == slot1 + capacity, gate1, 0.0)
    spread = jnp.concatenate(
        [
            jnp.where((place == slot0) | (place == slot1), 1.0, 0.0).astype(BF),
            jnp.where(place == slot0 + capacity, gate0, weighed).astype(BF),
        ],
        axis=0,
    )
    send[...] = tn(spread, values).astype(BF)


def split_matrix(rows, capacity):
    half = rows // 2
    r = iota((rows, rows), 0)
    c = iota((rows, rows), 1)
    kind = (r >= half).astype(jnp.int32)
    within = r - kind * half
    sender = ((within.astype(F32) + 0.5) * (1.0 / capacity)).astype(jnp.int32)
    source = within + (sender + kind) * capacity
    return (c == source).astype(BF)


def experts_kernel(capacity, group, cols, arrived, *refs):
    halves, refs = refs[:16], refs[16:]
    back, packed, left_out, mixed, w, xs, gs, acts, lefts, in_sem, w_sem, out_sem, back_sem = refs
    half = group // 2
    groups = arrived.shape[0] // group
    pieces, three, model = w.shape
    width = three // 3
    full = pieces * width
    parts = 4
    step = parts * width
    loads = [
        pltpu.make_async_copy(arrived.at[pl.ds(i * group, group)], mixed.at[pl.ds(i * group, group)], in_sem.at[i])
        for i in range(groups)
    ]
    held = [
        pltpu.make_async_copy(src, w.at[i // 2, pl.ds((i % 2) * (three // 2), three // 2)], w_sem.at[i]) for i, src in enumerate(halves)
    ]
    chunk = 2 * parts
    for copy in loads + held[:chunk]:
        copy.start()
    sel = split_matrix(group, capacity)
    for i in range(groups):
        loads[i].wait()
        if i == 1:
            for copy in held[chunk : 2 * chunk]:
                copy.start()
        both = nn(sel, mixed[i * group : (i + 1) * group, :]).astype(BF)
        xs[i * half : (i + 1) * half, :] = both[:half]
        gs[i * half : (i + 1) * half, :] = both[half:]
    outs = [pltpu.make_async_copy(src, packed.at[:, pl.ds(i * model, model)], out_sem.at[i]) for i, src in enumerate((xs, gs))]
    for c in range(pieces // parts):
        for copy in held[c * chunk : (c + 1) * chunk]:
            copy.wait()
        if c == 0:
            for copy in outs:
                copy.start()
        for copy in held[(c + 2) * chunk : (c + 3) * chunk]:
            copy.start()
        mine = slice(c * parts, (c + 1) * parts)
        x = xs[...]
        pre_gate = nt(x, w[mine, 0:width].reshape(step, model))
        pre_up = nt(x, w[mine, width : 2 * width].reshape(step, model))
        d_hidden = nt(gs[...], w[mine, 2 * width :].reshape(step, model))
        sig = jax.nn.sigmoid(pre_gate)
        active = pre_gate * sig
        hidden = active * pre_up
        d_gate = d_hidden * pre_up * sig * (1.0 + pre_gate * (1.0 - sig))
        d_up = d_hidden * active
        at = slice(c * step, (c + 1) * step)
        for m, part in enumerate((d_gate, d_up, hidden)):
            rounded = part.astype(BF)
            acts[m, :, at] = rounded
            if 2 * c < pieces // parts:
                lefts[m, at, :] = rounded.T
    mine = full // 2
    last = [pltpu.make_async_copy(lefts, left_out, out_sem.at[2])]
    for m in range(3):
        theirs = packed.at[:, pl.ds(2 * model + m * mine, mine)]
        last.append(pltpu.make_async_copy(acts.at[m, :, pl.ds(mine, mine)], theirs, out_sem.at[3 + m]))
    for copy in last:
        copy.start()
    outs += last
    for n in range(model // cols):
        at = slice(n * cols, (n + 1) * cols)
        y = nn(acts[2], w[:, 2 * width :, at].reshape(full, cols)).astype(BF)
        dx = nn(acts[0], w[:, 0:width, at].reshape(full, cols)) + nn(acts[1], w[:, width : 2 * width, at].reshape(full, cols))
        dx = dx.astype(BF)
        for i in range(groups):
            both = jnp.concatenate([y[i * half : (i + 1) * half], dx[i * half : (i + 1) * half]], axis=0)
            mixed[i * group : (i + 1) * group, at] = tn(sel, both).astype(BF)
        copy = pltpu.make_async_copy(mixed.at[:, pl.ds(n * cols, cols)], back.at[:, pl.ds(n * cols, cols)], back_sem.at[n])
        copy.start()
        outs.append(copy)
    for copy in outs:
        copy.wait()


def experts_call(arrived, halves, capacity):
    slots, width = arrived.shape
    three = 2 * halves[0].shape[0]
    pieces = len(halves) // 2
    full = pieces * three // 3
    rows = slots // 2
    group = 16 * capacity
    cols = width // 2
    hbm = pl.BlockSpec(memory_space=pl.ANY)
    return pl.pallas_call(
        functools.partial(experts_kernel, capacity, group, cols),
        in_specs=[hbm] * (1 + len(halves)),
        out_specs=[hbm] * 3,
        out_shape=(
            jax.ShapeDtypeStruct((slots, width), BF),
            jax.ShapeDtypeStruct((rows, 2 * width + 3 * full // 2), BF),
            jax.ShapeDtypeStruct((3, full // 2, rows), BF),
        ),
        scratch_shapes=[
            pltpu.VMEM((slots, width), BF),
            pltpu.VMEM((pieces, three, width), BF),
            pltpu.VMEM((rows, width), BF),
            pltpu.VMEM((rows, width), BF),
            pltpu.VMEM((3, rows, full), BF),
            pltpu.VMEM((3, full // 2, rows), BF),
            pltpu.SemaphoreType.DMA((slots // group,)),
            pltpu.SemaphoreType.DMA((len(halves),)),
            pltpu.SemaphoreType.DMA((6,)),
            pltpu.SemaphoreType.DMA((width // cols,)),
        ],
        compiler_params=pltpu.CompilerParams(vmem_limit_bytes=EXPERTS_LIMIT),
        cost_estimate=pl.CostEstimate(flops=12 * rows * full * width, bytes_accessed=8 * slots * width, transcendentals=rows * full),
        name="experts",
    )(arrived, *halves)


def sums_kernel(jobs, packed_a, left_a, packed_b, d0, d1, d2, d3, x, g, left, acts, p, in_sem, out_sem):
    rows = left_a.shape[2]
    model = x.shape[1]
    mine = left.shape[1]
    _, three, cols = p.shape
    width = three // 3
    def load(src, dst, n):
        return pltpu.make_async_copy(src, dst, in_sem.at[n])

    lefts = load(left_a, left.at[:, :, pl.ds(0, rows)], 0)
    theirs = [load(packed_b.at[:, pl.ds(2 * model + m * mine, mine)], acts.at[m], 1 + m) for m in range(3)]
    sides = []
    for j, side in enumerate((x, g)):
        for i, src in enumerate((packed_a, packed_b)):
            sides.append(load(src.at[:, pl.ds(j * model, model)], side.at[pl.ds(i * rows, rows)], 4 + 2 * j + i))
    for copy in theirs + [lefts] + sides:
        copy.start()
    for m in range(3):
        theirs[m].wait()
        left[m, :, rows:] = acts[m].T
    lefts.wait()
    outs = []
    dsts = (d0, d1, d2, d3)
    for m, right in enumerate((x, x, g)):
        for copy in (sides[0:2], [], sides[2:4])[m]:
            copy.wait()
        for i, (half, pair) in enumerate(jobs):
            lhs = jnp.concatenate([left[m, k * width : (k + 1) * width, :] for k in pair], axis=0)
            found = nn(lhs, right[:, half * cols : (half + 1) * cols]).astype(BF)
            for j in range(2):
                p[2 * i + j, m * width : (m + 1) * width, :] = found[j * width : (j + 1) * width]
                at = pl.ds(m * width, width)
                copy = pltpu.make_async_copy(p.at[2 * i + j, at], dsts[2 * i + j].at[at], out_sem.at[m, 2 * i + j])
                copy.start()
                outs.append(copy)
    for copy in outs:
        copy.wait()


def sums_call(packed, left, theirs, pieces, jobs, name):
    _, mine, rows = left.shape
    width = (packed.shape[1] - 3 * mine) // 2
    three = 3 * mine // pieces
    hbm = pl.BlockSpec(memory_space=pl.ANY)
    return pl.pallas_call(
        functools.partial(sums_kernel, jobs),
        in_specs=[hbm] * 3,
        out_specs=[hbm] * 4,
        out_shape=(jax.ShapeDtypeStruct((three, width // 2), BF),) * 4,
        scratch_shapes=[
            pltpu.VMEM((2 * rows, width), BF),
            pltpu.VMEM((2 * rows, width), BF),
            pltpu.VMEM((3, mine, 2 * rows), BF),
            pltpu.VMEM((3, rows, mine), BF),
            pltpu.VMEM((4, three, width // 2), BF),
            pltpu.SemaphoreType.DMA((8,)),
            pltpu.SemaphoreType.DMA((3, 4)),
        ],
        compiler_params=pltpu.CompilerParams(vmem_limit_bytes=SUMS_LIMIT),
        cost_estimate=pl.CostEstimate(flops=6 * rows * mine * width, bytes_accessed=16 * rows * width, transcendentals=0),
        name=name,
    )(packed, left, theirs)


def grads_kernel(q0a, q0b, q1a, q1b, q2a, q2b, o_gate, o_up, o_down, q, total, q_sem, o_sem):
    cols = q.shape[2] // 2
    loads = [
        pltpu.make_async_copy(src, q.at[k // 2, :, pl.ds((k % 2) * cols, cols)], q_sem.at[k]) for k, src in enumerate((q0a, q0b, q1a, q1b, q2a, q2b))
    ]
    for copy in loads:
        copy.start()
    for copy in loads:
        copy.wait()
    stores = []
    width = total.shape[1]
    for m, dst in enumerate((o_gate, o_up, o_down)):
        at = slice(m * width, (m + 1) * width)
        terms = [q[k, at].astype(F32) for k in range(3)]
        total[m] = terms[0] + terms[1] + terms[2]
        copy = pltpu.make_async_copy(total.at[m], dst.at[0], o_sem.at[m])
        copy.start()
        stores.append(copy)
    for copy in stores:
        copy.wait()


def after_kernel(capacity, table, scaled_in, notes, pool, norm, gain, out, grad, out_buf, grad_buf, sem):
    rows, model = scaled_in.shape
    factor = out.shape[0] // rows
    inv, gate0, gate1 = notes[:, 0:1], notes[:, 3:4], notes[:, 4:5]
    slot0, slot1 = notes[:, 1:2].astype(jnp.int32), notes[:, 2:3].astype(jnp.int32)
    place = iota((rows, table.shape[0]), 1)
    grad0, grad1 = slot0 + capacity, slot1 + capacity
    sel = jnp.concatenate(
        [
            jnp.where(place == slot0, 1.0, 0.0).astype(BF),
            jnp.where(place == slot1, 1.0, 0.0).astype(BF),
            jnp.where((place == grad0) | (place == grad1), 1.0, 0.0).astype(BF),
        ],
        axis=0,
    )
    band = rows // 3
    mix = jnp.concatenate([pick(band, factor, j) for j in range(factor)], axis=0)
    copies = []

    def store(values, scale, buf, dst, first):
        for i in range(3):
            part = values[i * band : (i + 1) * band]
            blocks = jnp.concatenate([(scale[j : j + 1, :] * part).astype(BF) for j in range(factor)], axis=0)
            at = slice(i * band * factor, (i + 1) * band * factor)
            buf[at, :] = tn(mix, blocks).astype(BF)
            span = pl.ds(i * band * factor, band * factor)
            copy = pltpu.make_async_copy(buf.at[span], dst.at[span], sem.at[first + i])
            copy.start()
            copies.append(copy)

    found = nn(sel, table[...])
    mixture = gate0 * found[:rows] + gate1 * found[rows : 2 * rows]
    store(mixture, gain, out_buf, out, 0)
    d_scaled = found[2 * rows :] * norm[...]
    scaled = scaled_in[...]
    d_short = inv * (d_scaled - scaled * jnp.mean(d_scaled * scaled, axis=1, keepdims=True))
    store(d_short, pool, grad_buf, grad, 3)
    for copy in copies:
        copy.wait()


def shards(
    tokens,
    cotangent,
    expert_ids,
    votes,
    pool_weight,
    norm_gain,
    up_gain,
    gate_weight,
    up_weight,
    down_weight,
):
    ring = lax.axis_size("y")
    experts = lax.axis_size("z") * lax.axis_size("x")
    rows, top = expert_ids.shape
    width = tokens.shape[1]
    hidden = gate_weight.shape[1]
    capacity = 2 * rows * top // experts
    slots = 2 * experts * capacity
    params = pltpu.CompilerParams(vmem_limit_bytes=EDGE_LIMIT)
    vmem = pl.BlockSpec(memory_space=pltpu.VMEM)
    hbm = pl.BlockSpec(memory_space=pl.ANY)
    norm = norm_gain[None]
    ids, counts = expert_ids.T, votes.T

    def move(a, k):
        return lax.ppermute(a, "y", [(i, (i + k) % ring) for i in range(ring)])

    def swap(a):
        return lax.ppermute(a, "core", [(0, 1), (1, 0)])

    def exchange(a):
        return lax.all_to_all(a, ("z", "x"), split_axis=0, concat_axis=0, tiled=True)

    up, down = 1, ring - 1
    h0, h1 = pl.pallas_call(
        pack_kernel,
        in_specs=[hbm] * 3,
        out_specs=[hbm] * 2,
        out_shape=(jax.ShapeDtypeStruct((3 * hidden // 2, width), BF),) * 2,
        scratch_shapes=[pltpu.VMEM((3 * hidden, width), BF), pltpu.SemaphoreType.DMA((3,)), pltpu.SemaphoreType.DMA((2,))],
        compiler_params=params,
        name="pack",
    )(gate_weight, up_weight, down_weight)
    u0, d1 = move(h0, up), move(h1, down)
    t0, t1 = move(u0, up), move(d1, down)
    u1, d0 = move(h1, up), move(h0, down)
    halves = [h0, h1, u0, u1, t0, t1, d0, d1]
    least = jnp.asarray(jnp.finfo(BF).min, BF)
    halves = [jnp.maximum(h0, least), jnp.maximum(h1, least), *halves[2:]] + [swap(a) for a in halves]

    send, scaled, notes = pl.pallas_call(
        functools.partial(before_kernel, experts, capacity),
        out_shape=(
            jax.ShapeDtypeStruct((slots, width), BF),
            jax.ShapeDtypeStruct((rows, width), F32),
            jax.ShapeDtypeStruct((rows, 128), F32),
        ),
        compiler_params=params,
        name="before",
    )(tokens, cotangent, ids, counts, pool_weight, norm, up_gain)

    arrived = exchange(send)
    back, packed, left = experts_call(arrived, halves, capacity)
    theirs = swap(packed)
    returned = exchange(back)
    p2a, p3a, p1b, p2b = sums_call(packed, left, theirs, ring, ((0, (2, 3)), (1, (1, 2))), "sums_far")
    p0a, p1a, p3b, p0b = sums_call(packed, left, theirs, ring, ((0, (0, 1)), (1, (3, 0))), "sums_near")
    r1b, r3a = move(p1b, down), move(p3a, up)
    r1a = move(p1a + move(p2a, down), down)
    r3b = move(p3b + move(p2b, up), up)
    parts = (p0a, p0b, r1a, r1b, r3a, r3b)

    held = jax.ShapeDtypeStruct((1, hidden, width), F32)
    grads = pl.pallas_call(
        grads_kernel,
        in_specs=[hbm] * 6,
        out_specs=[hbm] * 3,
        out_shape=(held, held, held),
        scratch_shapes=[
            pltpu.VMEM((3, 3 * hidden, width), BF),
            pltpu.VMEM((3, hidden, width), F32),
            pltpu.SemaphoreType.DMA((6,)),
            pltpu.SemaphoreType.DMA((3,)),
        ],
        compiler_params=params,
        name="grads",
    )(*parts)

    shape = jax.ShapeDtypeStruct(tokens.shape, BF)
    layer_out, tokens_grad = pl.pallas_call(
        functools.partial(after_kernel, capacity),
        in_specs=[vmem] * 6,
        out_specs=[hbm] * 2,
        out_shape=(shape, shape),
        scratch_shapes=[pltpu.VMEM(tokens.shape, BF), pltpu.VMEM(tokens.shape, BF), pltpu.SemaphoreType.DMA((6,))],
        compiler_params=pltpu.CompilerParams(vmem_limit_bytes=AFTER_LIMIT),
        name="after",
    )(returned, scaled, notes, pool_weight, norm, up_gain)
    return (layer_out, tokens_grad, *grads)


def solution(mesh):
    sizes = (mesh.shape["dp"] // 2, 2, mesh.shape["expert"] // 4, 4)
    mesh = jax.sharding.Mesh(mesh.devices.reshape(sizes), ("y", "core", "z", "x"))
    rows = P(("y", "core", "z", "x"), None)
    held = P(("z", "x"), ("y", "core"), None)
    return jax.shard_map(
        shards,
        mesh=mesh,
        in_specs=(rows, rows, rows, rows, P(), P(), P(), held, held, held),
        out_specs=(rows, rows, held, held, held),
        check_vma=False,
    )
```

```python
import functools

import jax
import jax.numpy as jnp
from jax import lax
from jax.experimental import pallas as pl
from jax.experimental.pallas import tpu as pltpu
from jax.sharding import PartitionSpec as P

BF = jnp.bfloat16
F32 = jnp.float32
MIB = 1024 * 1024
BLOCKS = 4
EDGE_LIMIT = 60 * MIB
AFTER_LIMIT = 52 * MIB
EXPERTS_LIMIT = 51 * MIB
SUMS_LIMIT = 60 * MIB


def nn(a, b):
    return jnp.dot(a, b, preferred_element_type=F32)


def nt(a, b):
    return lax.dot_general(a, b, (((1,), (1,)), ((), ())), preferred_element_type=F32)


def tn(a, b):
    return lax.dot_general(a, b, (((0,), (0,)), ((), ())), preferred_element_type=F32)


def iota(shape, axis):
    return lax.broadcasted_iota(jnp.int32, shape, axis)


def slots_and_gates(ids_ref, votes_ref, experts, capacity):
    rows = ids_ref.shape[1]
    ids = ids_ref[...].astype(F32).T.astype(jnp.int32)
    first, second = ids[:, 0:1], ids[:, 1:2]
    names = iota((rows, experts), 1)
    hot0 = (names == first).astype(F32)
    hot1 = (names == second).astype(F32)
    earlier = (iota((rows, rows), 0) > iota((rows, rows), 1)).astype(BF)
    before = nn(earlier, (hot0 + hot1).astype(BF))
    rank0 = jnp.sum(before * hot0, axis=1, keepdims=True).astype(jnp.int32)
    rank1 = jnp.sum(before * hot1, axis=1, keepdims=True).astype(jnp.int32)
    votes = votes_ref[...].astype(F32).T
    total = votes[:, 0:1] + votes[:, 1:2]
    slot0 = first * (2 * capacity) + rank0
    slot1 = second * (2 * capacity) + rank1
    return slot0, slot1, votes[:, 0:1] / total, votes[:, 1:2] / total


def pick(rows, factor, j):
    shape = (rows, rows * factor)
    return (iota(shape, 1) == iota(shape, 0) * factor + j).astype(BF)


def pack_kernel(w_gate, w_up, w_down, first, second, held, in_sem, out_sem):
    width = w_gate.shape[1]
    half = first.shape[0]
    loads = [pltpu.make_async_copy(src.at[0], held.at[pl.ds(m * width, width)], in_sem.at[m]) for m, src in enumerate((w_gate, w_up, w_down))]
    stores = [pltpu.make_async_copy(held.at[pl.ds(h * half, half)], dst, out_sem.at[h]) for h, dst in enumerate((first, second))]
    for copy in loads:
        copy.start()
    for copy in loads[:2]:
        copy.wait()
    stores[0].start()
    loads[2].wait()
    stores[1].start()
    for copy in stores:
        copy.wait()


def before_kernel(experts, capacity, tokens, cotangent, ids, votes, pool, norm, gain, send, scaled_out, notes, kept, out, sem):
    rows = ids.shape[1]
    factor = tokens.shape[0] // rows
    slot0, slot1, gate0, gate1 = slots_and_gates(ids, votes, experts, capacity)
    band = rows // 3
    sel = jnp.concatenate([pick(band, factor, j) for j in range(factor)], axis=0)
    shorts, mixes = [], []
    for i in range(3):
        at = slice(i * band * factor, (i + 1) * band * factor)
        tok, cot = nn(sel, tokens[at, :]), nn(sel, cotangent[at, :])
        short = d_mix = None
        for j in range(factor):
            a = tok[j * band : (j + 1) * band] * pool[j : j + 1, :]
            b = cot[j * band : (j + 1) * band] * gain[j : j + 1, :]
            short = a if short is None else short + a
            d_mix = b if d_mix is None else d_mix + b
        shorts.append(short)
        mixes.append(d_mix)
    short = jnp.concatenate(shorts, axis=0)
    d_mix = jnp.concatenate(mixes, axis=0)
    inv = lax.rsqrt(jnp.mean(short * short, axis=1, keepdims=True) + 1e-06)
    scaled = short * inv
    kept[...] = scaled
    copies = [pltpu.make_async_copy(kept, scaled_out, sem.at[0])]
    copies[0].start()
    lane = iota(notes.shape, 1)
    noted = inv
    for n, column in enumerate((slot0.astype(F32), slot1.astype(F32), gate0, gate1)):
        noted = jnp.where(lane == n + 1, column, noted)
    notes[...] = noted
    values = jnp.concatenate([(scaled * norm[...]).astype(BF), d_mix.astype(BF)], axis=0)
    place = iota((rows, out.shape[0]), 1)
    weighed = jnp.where(place == slot1 + capacity, gate1, 0.0)
    spread = jnp.concatenate(
        [
            jnp.where((place == slot0) | (place == slot1), 1.0, 0.0).astype(BF),
            jnp.where(place == slot0 + capacity, gate0, weighed).astype(BF),
        ],
        axis=0,
    )
    blocks = sem.shape[0] - 1
    cols = out.shape[1] // blocks
    for n in range(blocks):
        at = slice(n * cols, (n + 1) * cols)
        out[:, at] = tn(spread, values[:, at]).astype(BF)
        copy = pltpu.make_async_copy(out.at[:, pl.ds(n * cols, cols)], send.at[:, pl.ds(n * cols, cols)], sem.at[1 + n])
        copy.start()
        copies.append(copy)
    for copy in copies:
        copy.wait()


def split_matrix(rows, capacity):
    half = rows // 2
    r = iota((rows, rows), 0)
    c = iota((rows, rows), 1)
    kind = (r >= half).astype(jnp.int32)
    within = r - kind * half
    sender = ((within.astype(F32) + 0.5) * (1.0 / capacity)).astype(jnp.int32)
    source = within + (sender + kind) * capacity
    return (c == source).astype(BF)


def experts_kernel(capacity, group, cols, arrived, *refs):
    halves, refs = refs[:16], refs[16:]
    back, packed, left_out, mixed, w, xs, gs, acts, lefts, in_sem, w_sem, out_sem, back_sem = refs
    half = group // 2
    groups = arrived.shape[0] // group
    pieces, three, model = w.shape
    width = three // 3
    full = pieces * width
    parts = 4
    step = parts * width
    loads = [
        pltpu.make_async_copy(arrived.at[pl.ds(i * group, group)], mixed.at[pl.ds(i * group, group)], in_sem.at[i])
        for i in range(groups)
    ]
    held = [
        pltpu.make_async_copy(src, w.at[i // 2, pl.ds((i % 2) * (three // 2), three // 2)], w_sem.at[i]) for i, src in enumerate(halves)
    ]
    chunk = 2 * parts
    for copy in loads + held[:chunk]:
        copy.start()
    sel = split_matrix(group, capacity)
    for i in range(groups):
        loads[i].wait()
        if i == 1:
            for copy in held[chunk : 2 * chunk]:
                copy.start()
        both = nn(sel, mixed[i * group : (i + 1) * group, :]).astype(BF)
        xs[i * half : (i + 1) * half, :] = both[:half]
        gs[i * half : (i + 1) * half, :] = both[half:]
    outs = [pltpu.make_async_copy(src, packed.at[:, pl.ds(i * model, model)], out_sem.at[i]) for i, src in enumerate((xs, gs))]
    for c in range(pieces // parts):
        for copy in held[c * chunk : (c + 1) * chunk]:
            copy.wait()
        if c == 0:
            for copy in outs:
                copy.start()
        for copy in held[(c + 2) * chunk : (c + 3) * chunk]:
            copy.start()
        mine = slice(c * parts, (c + 1) * parts)
        x = xs[...]
        pre_gate = nt(x, w[mine, 0:width].reshape(step, model))
        pre_up = nt(x, w[mine, width : 2 * width].reshape(step, model))
        d_hidden = nt(gs[...], w[mine, 2 * width :].reshape(step, model))
        sig = jax.nn.sigmoid(pre_gate)
        active = pre_gate * sig
        hidden = active * pre_up
        d_gate = d_hidden * pre_up * sig * (1.0 + pre_gate * (1.0 - sig))
        d_up = d_hidden * active
        at = slice(c * step, (c + 1) * step)
        for m, part in enumerate((d_gate, d_up, hidden)):
            rounded = part.astype(BF)
            acts[m, :, at] = rounded
            if 2 * c < pieces // parts:
                lefts[m, at, :] = rounded.T
    mine = full // 2
    last = [pltpu.make_async_copy(lefts, left_out, out_sem.at[2])]
    for m in range(3):
        theirs = packed.at[:, pl.ds(2 * model + m * mine, mine)]
        last.append(pltpu.make_async_copy(acts.at[m, :, pl.ds(mine, mine)], theirs, out_sem.at[3 + m]))
    for copy in last:
        copy.start()
    outs += last
    for n in range(model // cols):
        at = slice(n * cols, (n + 1) * cols)
        y = nn(acts[2], w[:, 2 * width :, at].reshape(full, cols)).astype(BF)
        dx = nn(acts[0], w[:, 0:width, at].reshape(full, cols)) + nn(acts[1], w[:, width : 2 * width, at].reshape(full, cols))
        dx = dx.astype(BF)
        for i in range(groups):
            both = jnp.concatenate([y[i * half : (i + 1) * half], dx[i * half : (i + 1) * half]], axis=0)
            mixed[i * group : (i + 1) * group, at] = tn(sel, both).astype(BF)
        copy = pltpu.make_async_copy(mixed.at[:, pl.ds(n * cols, cols)], back.at[:, pl.ds(n * cols, cols)], back_sem.at[n])
        copy.start()
        outs.append(copy)
    for copy in outs:
        copy.wait()


def experts_call(arrived, halves, capacity):
    slots, width = arrived.shape
    three = 2 * halves[0].shape[0]
    pieces = len(halves) // 2
    full = pieces * three // 3
    rows = slots // 2
    group = 16 * capacity
    cols = width // 2
    hbm = pl.BlockSpec(memory_space=pl.ANY)
    return pl.pallas_call(
        functools.partial(experts_kernel, capacity, group, cols),
        in_specs=[hbm] * (1 + len(halves)),
        out_specs=[hbm] * 3,
        out_shape=(
            jax.ShapeDtypeStruct((slots, width), BF),
            jax.ShapeDtypeStruct((rows, 2 * width + 3 * full // 2), BF),
            jax.ShapeDtypeStruct((3, full // 2, rows), BF),
        ),
        scratch_shapes=[
            pltpu.VMEM((slots, width), BF),
            pltpu.VMEM((pieces, three, width), BF),
            pltpu.VMEM((rows, width), BF),
            pltpu.VMEM((rows, width), BF),
            pltpu.VMEM((3, rows, full), BF),
            pltpu.VMEM((3, full // 2, rows), BF),
            pltpu.SemaphoreType.DMA((slots // group,)),
            pltpu.SemaphoreType.DMA((len(halves),)),
            pltpu.SemaphoreType.DMA((6,)),
            pltpu.SemaphoreType.DMA((width // cols,)),
        ],
        compiler_params=pltpu.CompilerParams(vmem_limit_bytes=EXPERTS_LIMIT),
        cost_estimate=pl.CostEstimate(flops=12 * rows * full * width, bytes_accessed=8 * slots * width, transcendentals=rows * full),
        name="experts",
    )(arrived, *halves)


def sums_kernel(jobs, packed_a, left_a, packed_b, d0, d1, d2, d3, x, g, left, acts, p, in_sem, out_sem):
    rows = left_a.shape[2]
    model = x.shape[1]
    mine = left.shape[1]
    _, three, cols = p.shape
    width = three // 3
    def load(src, dst, n):
        return pltpu.make_async_copy(src, dst, in_sem.at[n])

    lefts = load(left_a, left.at[:, :, pl.ds(0, rows)], 0)
    theirs = [load(packed_b.at[:, pl.ds(2 * model + m * mine, mine)], acts.at[m], 1 + m) for m in range(3)]
    sides = []
    for j, side in enumerate((x, g)):
        for i, src in enumerate((packed_a, packed_b)):
            sides.append(load(src.at[:, pl.ds(j * model, model)], side.at[pl.ds(i * rows, rows)], 4 + 2 * j + i))
    for copy in theirs + [lefts] + sides:
        copy.start()
    for m in range(3):
        theirs[m].wait()
        left[m, :, rows:] = acts[m].T
    lefts.wait()
    outs = []
    dsts = (d0, d1, d2, d3)
    for m, right in enumerate((x, x, g)):
        for copy in (sides[0:2], [], sides[2:4])[m]:
            copy.wait()
        for i, (half, pair) in enumerate(jobs):
            lhs = jnp.concatenate([left[m, k * width : (k + 1) * width, :] for k in pair], axis=0)
            found = nn(lhs, right[:, half * cols : (half + 1) * cols]).astype(BF)
            for j in range(2):
                p[2 * i + j, m * width : (m + 1) * width, :] = found[j * width : (j + 1) * width]
                at = pl.ds(m * width, width)
                copy = pltpu.make_async_copy(p.at[2 * i + j, at], dsts[2 * i + j].at[at], out_sem.at[m, 2 * i + j])
                copy.start()
                outs.append(copy)
    for copy in outs:
        copy.wait()


def sums_call(packed, left, theirs, pieces, jobs, name):
    _, mine, rows = left.shape
    width = (packed.shape[1] - 3 * mine) // 2
    three = 3 * mine // pieces
    hbm = pl.BlockSpec(memory_space=pl.ANY)
    return pl.pallas_call(
        functools.partial(sums_kernel, jobs),
        in_specs=[hbm] * 3,
        out_specs=[hbm] * 4,
        out_shape=(jax.ShapeDtypeStruct((three, width // 2), BF),) * 4,
        scratch_shapes=[
            pltpu.VMEM((2 * rows, width), BF),
            pltpu.VMEM((2 * rows, width), BF),
            pltpu.VMEM((3, mine, 2 * rows), BF),
            pltpu.VMEM((3, rows, mine), BF),
            pltpu.VMEM((4, three, width // 2), BF),
            pltpu.SemaphoreType.DMA((8,)),
            pltpu.SemaphoreType.DMA((3, 4)),
        ],
        compiler_params=pltpu.CompilerParams(vmem_limit_bytes=SUMS_LIMIT),
        cost_estimate=pl.CostEstimate(flops=6 * rows * mine * width, bytes_accessed=16 * rows * width, transcendentals=0),
        name=name,
    )(packed, left, theirs)


def grads_kernel(q0a, q0b, q1a, q1b, q2a, q2b, o_gate, o_up, o_down, q, total, q_sem, o_sem):
    cols = q.shape[2] // 2
    loads = [
        pltpu.make_async_copy(src, q.at[k // 2, :, pl.ds((k % 2) * cols, cols)], q_sem.at[k]) for k, src in enumerate((q0a, q0b, q1a, q1b, q2a, q2b))
    ]
    for copy in loads:
        copy.start()
    for copy in loads:
        copy.wait()
    stores = []
    width = total.shape[1]
    for m, dst in enumerate((o_gate, o_up, o_down)):
        at = slice(m * width, (m + 1) * width)
        terms = [q[k, at].astype(F32) for k in range(3)]
        total[m] = terms[0] + terms[1] + terms[2]
        copy = pltpu.make_async_copy(total.at[m], dst.at[0], o_sem.at[m])
        copy.start()
        stores.append(copy)
    for copy in stores:
        copy.wait()


def after_kernel(capacity, table, scaled_in, notes, pool, norm, gain, out, grad, out_buf, grad_buf, sem):
    rows, model = scaled_in.shape
    factor = out.shape[0] // rows
    inv, gate0, gate1 = notes[:, 0:1], notes[:, 3:4], notes[:, 4:5]
    slot0, slot1 = notes[:, 1:2].astype(jnp.int32), notes[:, 2:3].astype(jnp.int32)
    place = iota((rows, table.shape[0]), 1)
    grad0, grad1 = slot0 + capacity, slot1 + capacity
    sel = jnp.concatenate(
        [
            jnp.where(place == slot0, 1.0, 0.0).astype(BF),
            jnp.where(place == slot1, 1.0, 0.0).astype(BF),
            jnp.where((place == grad0) | (place == grad1), 1.0, 0.0).astype(BF),
        ],
        axis=0,
    )
    band = rows // 3
    mix = jnp.concatenate([pick(band, factor, j) for j in range(factor)], axis=0)
    copies = []

    def store(values, scale, buf, dst, first):
        for i in range(3):
            part = values[i * band : (i + 1) * band]
            blocks = jnp.concatenate([(scale[j : j + 1, :] * part).astype(BF) for j in range(factor)], axis=0)
            at = slice(i * band * factor, (i + 1) * band * factor)
            buf[at, :] = tn(mix, blocks).astype(BF)
            span = pl.ds(i * band * factor, band * factor)
            copy = pltpu.make_async_copy(buf.at[span], dst.at[span], sem.at[first + i])
            copy.start()
            copies.append(copy)

    found = nn(sel, table[...])
    mixture = gate0 * found[:rows] + gate1 * found[rows : 2 * rows]
    store(mixture, gain, out_buf, out, 0)
    d_scaled = found[2 * rows :] * norm[...]
    scaled = scaled_in[...]
    d_short = inv * (d_scaled - scaled * jnp.mean(d_scaled * scaled, axis=1, keepdims=True))
    store(d_short, pool, grad_buf, grad, 3)
    for copy in copies:
        copy.wait()


def shards(
    tokens,
    cotangent,
    expert_ids,
    votes,
    pool_weight,
    norm_gain,
    up_gain,
    gate_weight,
    up_weight,
    down_weight,
):
    ring = lax.axis_size("y")
    experts = lax.axis_size("z") * lax.axis_size("x")
    rows, top = expert_ids.shape
    width = tokens.shape[1]
    hidden = gate_weight.shape[1]
    capacity = 2 * rows * top // experts
    slots = 2 * experts * capacity
    params = pltpu.CompilerParams(vmem_limit_bytes=EDGE_LIMIT)
    vmem = pl.BlockSpec(memory_space=pltpu.VMEM)
    hbm = pl.BlockSpec(memory_space=pl.ANY)
    norm = norm_gain[None]
    ids, counts = expert_ids.T, votes.T

    def move(a, k):
        return lax.ppermute(a, "y", [(i, (i + k) % ring) for i in range(ring)])

    def swap(a):
        return lax.ppermute(a, "core", [(0, 1), (1, 0)])

    def exchange(a):
        return lax.all_to_all(a, ("z", "x"), split_axis=0, concat_axis=0, tiled=True)

    up, down = 1, ring - 1
    h0, h1 = pl.pallas_call(
        pack_kernel,
        in_specs=[hbm] * 3,
        out_specs=[hbm] * 2,
        out_shape=(jax.ShapeDtypeStruct((3 * hidden // 2, width), BF),) * 2,
        scratch_shapes=[pltpu.VMEM((3 * hidden, width), BF), pltpu.SemaphoreType.DMA((3,)), pltpu.SemaphoreType.DMA((2,))],
        compiler_params=params,
        name="pack",
    )(gate_weight, up_weight, down_weight)
    u0, d1 = move(h0, up), move(h1, down)
    t0, t1 = move(u0, up), move(d1, down)
    u1, d0 = move(h1, up), move(h0, down)
    halves = [h0, h1, u0, u1, t0, t1, d0, d1]
    least = jnp.asarray(jnp.finfo(BF).min, BF)
    halves = [jnp.maximum(h0, least), jnp.maximum(h1, least), *halves[2:]] + [swap(a) for a in halves]

    send, scaled, notes = pl.pallas_call(
        functools.partial(before_kernel, experts, capacity),
        in_specs=[vmem] * 7,
        out_specs=[hbm, hbm, vmem],
        out_shape=(
            jax.ShapeDtypeStruct((slots, width), BF),
            jax.ShapeDtypeStruct((rows, width), F32),
            jax.ShapeDtypeStruct((rows, 128), F32),
        ),
        scratch_shapes=[pltpu.VMEM((rows, width), F32), pltpu.VMEM((slots, width), BF), pltpu.SemaphoreType.DMA((BLOCKS + 1,))],
        compiler_params=params,
        name="before",
    )(tokens, cotangent, ids, counts, pool_weight, norm, up_gain)

    arrived = exchange(send)
    back, packed, left = experts_call(arrived, halves, capacity)
    theirs = swap(packed)
    returned = exchange(back)
    p2a, p3a, p1b, p2b = sums_call(packed, left, theirs, ring, ((0, (2, 3)), (1, (1, 2))), "sums_far")
    p0a, p1a, p3b, p0b = sums_call(packed, left, theirs, ring, ((0, (0, 1)), (1, (3, 0))), "sums_near")
    r1b, r3a = move(p1b, down), move(p3a, up)
    r1a = move(p1a + move(p2a, down), down)
    r3b = move(p3b + move(p2b, up), up)
    parts = (p0a, p0b, r1a, r1b, r3a, r3b)

    held = jax.ShapeDtypeStruct((1, hidden, width), F32)
    grads = pl.pallas_call(
        grads_kernel,
        in_specs=[hbm] * 6,
        out_specs=[hbm] * 3,
        out_shape=(held, held, held),
        scratch_shapes=[
            pltpu.VMEM((3, 3 * hidden, width), BF),
            pltpu.VMEM((3, hidden, width), F32),
            pltpu.SemaphoreType.DMA((6,)),
            pltpu.SemaphoreType.DMA((3,)),
        ],
        compiler_params=params,
        name="grads",
    )(*parts)

    shape = jax.ShapeDtypeStruct(tokens.shape, BF)
    layer_out, tokens_grad = pl.pallas_call(
        functools.partial(after_kernel, capacity),
        in_specs=[vmem] * 6,
        out_specs=[hbm] * 2,
        out_shape=(shape, shape),
        scratch_shapes=[pltpu.VMEM(tokens.shape, BF), pltpu.VMEM(tokens.shape, BF), pltpu.SemaphoreType.DMA((6,))],
        compiler_params=pltpu.CompilerParams(vmem_limit_bytes=AFTER_LIMIT),
        name="after",
    )(returned, scaled, notes, pool_weight, norm, up_gain)
    return (layer_out, tokens_grad, *grads)


def solution(mesh):
    sizes = (mesh.shape["dp"] // 2, 2, mesh.shape["expert"] // 4, 4)
    mesh = jax.sharding.Mesh(mesh.devices.reshape(sizes), ("y", "core", "z", "x"))
    rows = P(("y", "core", "z", "x"), None)
    held = P(("z", "x"), ("y", "core"), None)
    return jax.shard_map(
        shards,
        mesh=mesh,
        in_specs=(rows, rows, rows, rows, P(), P(), P(), held, held, held),
        out_specs=(rows, rows, held, held, held),
        check_vma=False,
    )
```
